512 devices in a mesh: grp: 4 (over y), cell: 128 (over z, x, core).
Axes of the slice: x: 4, y: 4, z: 16, core: 2. Of those that a mesh axis runs over, the one named last changes fastest.
Arguments:
- block_ids: int32 [16384, 64, 1], P(('grp', 'cell')), may hold values from 0 to 511; in each aligned block of 2048 rows (0 to 2047, 2048 to 4095, ..., all dimensions but the last counted through in order) at most 8 rows name the same one
- positions: float32 [3, 16384, 64], P(None, ('grp', 'cell')), may hold values from -1 to 1
- spacing: float32 [16384, 64], P(('grp', 'cell')), may hold values from 0.01 to 0.06
- lengths: int32 [16384], P(('grp', 'cell')), may hold values from 16 to 64
- color_grad: float32 [3, 16384], P(None, ('grp', 'cell')), may hold values from -6 to 6
- first_weight: bfloat16 [512, 96, 256], P('cell'), may hold values from -0.625 to 0.625
- first_bias: float32 [512, 256], P('cell'), may hold values from -3 to 3
- second_weight: bfloat16 [512, 256, 256], P('cell'), may hold values from -0.375 to 0.375
- second_bias: float32 [512, 256], P('cell'), may hold values from -3 to 3
- third_weight: bfloat16 [512, 4, 256], P('cell'), may hold values from -0.375 to 0.375
- third_bias: float32 [512, 4], P('cell'), may hold values from -4 to 4
Outputs:
- grad_first_weight: float32 [512, 96, 256], P('cell')
- grad_first_bias: float32 [512, 256], P('cell')
- grad_second_weight: float32 [512, 256, 256], P('cell')
- grad_second_bias: float32 [512, 256], P('cell')
- grad_third_weight: float32 [512, 4, 256], P('cell')
- grad_third_bias: float32 [512, 4], P('cell')
The draws below stay inside these ranges and needn't reach their ends.
Inputs may be any that keep to these rules, and one draw needn't show every extreme that they name: `block_ids`: the 32 rays of one device hold at most 8 samples of any one block, and exactly 8 of some block on some device.
All inputs are finite; a program needn't handle non-finite values.
Results may differ from the reference program's by a relative error of at most 0.0095.
Values may be sent and summed in bfloat16 or wider, within the bound.
A program may use at most 64 MiB of HBM per device.

```python
import math
import jax
import jax.numpy as jnp
import numpy as np
from jax import lax

LEVELS = 16
ENC = 96
HID = 256
RAW_CH = 4
SAMP = 64
RAYS_DEV = 32
BLOCKS = 512
RAYS = 16384
CAP = 8
N_GRP = 4
N_CELL = 128


def plant(result, own_key, low, largest):
    dims = result.shape
    index_at = [jax.random.randint(jax.random.fold_in(own_key, axis), (), 0, dims[axis]) for axis in range(len(dims))]
    result = result.at[tuple(index_at)].set(low)
    longest = dims.index(max(dims))
    index_at[longest] = (index_at[longest] + 1) % dims[longest]
    return result.at[tuple(index_at)].set(largest)


def level_of(own_key, dims, shards, low, top_value):
    level, own = 1.0, jax.random.fold_in(own_key, 6)
    for position, parts in shards:
        heights = jnp.exp(jax.random.uniform(jax.random.fold_in(own, position), (parts,), jnp.float32, low / len(shards), top_value / len(shards)))
        level = level * jnp.repeat(heights, dims[position] // parts).reshape([-1 if axis == position else 1 for axis in range(len(dims))])
    return level


def shared_out(own_key, own, number, rows, amount, top, reach, lean):
    order = jax.random.permutation(own_key, amount)
    packed, ordinary = portions_of(amount, rows * top, reach, lean, True), portions_of(amount, rows * top, reach, lean, False)
    places = jnp.arange(amount)

    def named(tallies, offset_by):
        used = int((tallies > 0).sum())
        fixed = max(1, used // 4)
        moved = fixed + (places - fixed + offset_by * (used - fixed)) % max(1, amount - fixed)
        return jnp.zeros((amount,), jnp.int32).at[order[jnp.where(places < fixed, places, moved)]].set(jnp.asarray(tallies, jnp.int32))

    tallies = jnp.where(number % 4 == 0, named(packed, number // 4), named(ordinary, number - number // 4 - 1))
    mixed = jax.random.permutation(jax.random.fold_in(own, 3), amount)
    giver, taker = mixed[0:amount // 2 * 2:2], mixed[1:amount // 2 * 2:2]
    margin = jnp.minimum(tallies[giver] - 1, reach - tallies[taker]) // 2
    margin = jnp.where((giver == order[0]) | (taker == order[0]) | (tallies[taker] == 0), 0, jnp.maximum(margin, 0))
    moved = jax.random.randint(jax.random.fold_in(own, 4), (amount // 2,), 0, 1 << 20) % (margin + 1)
    tallies = tallies.at[giver].add(-moved).at[taker].add(moved)
    labels = jnp.searchsorted(jnp.cumsum(tallies), jnp.arange(rows * top), side="right").astype(jnp.int32)
    listing = labels.reshape(top, rows).T
    listing = listing[jax.random.permutation(jax.random.fold_in(own, 1), rows)]
    offset_by = jax.random.randint(jax.random.fold_in(own, 2), (rows, 1), 0, top)
    return jnp.take_along_axis(listing, (jnp.arange(top)[None, :] + offset_by) % top, axis=1)


def portions_of(count, total, bound, skew, full):
    weights = [(1 << 20) // math.isqrt(standing ** skew) + 1 for standing in range(1, count + 1)]
    largest = bound if full else min(bound, max(-(-total // count), total * weights[0] // sum(weights)))
    least = 1 if total - largest >= count - 1 else 0
    holding, rest = [largest] + [least] * (count - 1), total - largest - least * (count - 1)
    while rest > 0:
        candidates = [i for i in range(1, count) if holding[i] < largest] or [i for i in range(1, count) if holding[i] < bound]
        whole, left = sum([weights[i] for i in candidates]), rest
        for i in candidates:
            more = min(bound - holding[i], max(1, left * weights[i] // whole), rest)
            holding[i] = holding[i] + more
            rest = rest - more
    return np.array(holding)


def noise(own_key, extent, deviation, most, cuts=(), kind=jnp.bfloat16):
    level = level_of(own_key, extent, cuts, -0.22, 0.18) if cuts else 1.0
    entries = jax.random.normal(own_key, extent, jnp.float32) * deviation * level
    return jnp.minimum(jnp.maximum(entries, -most), most).astype(kind)


def setup_inputs(seed: int = 0) -> dict:
    keys = jax.random.split(jax.random.key(seed), 12)
    block_ids_keys = jax.random.split(jax.random.fold_in(keys[0], 1), RAYS * SAMP // (RAYS_DEV * SAMP))
    block_ids_turns = jax.random.permutation(jax.random.fold_in(keys[0], 3), RAYS * SAMP // (RAYS_DEV * SAMP))
    block_ids = jax.vmap(lambda own, number: shared_out(jax.random.fold_in(keys[0], 2), own, number, RAYS_DEV * SAMP, BLOCKS, 1, CAP, 2))(block_ids_keys, block_ids_turns).reshape((RAYS, SAMP, 1))
    positions = jnp.clip(jax.random.uniform(keys[1], (3, RAYS, SAMP), jnp.float32, -1.0, 1.0) * level_of(keys[1], (3, RAYS, SAMP), ((1, 512),), -0.4, 0.0), -1.0, 1.0)
    spacing = jnp.clip(jnp.exp(math.log(0.06) - 1.7917595 * jax.random.uniform(keys[2], (RAYS, SAMP), jnp.float32) ** level_of(keys[2], (RAYS, SAMP), ((0, 512),), -0.2, 0.2)), 0.01, 0.06)
    lengths = plant(jax.random.randint(keys[3], (RAYS,), SAMP // 4, SAMP + 1), jax.random.fold_in(keys[3], 1), SAMP // 4, SAMP).astype(jnp.int32)
    color_grad = noise(keys[4], (3, RAYS), 1.0, 6.0, ((1, 512),), jnp.float32)
    first_weight = noise(keys[5], (BLOCKS, ENC, HID), ENC ** -0.5, 0.625, ((0, 128),))
    first_bias = noise(keys[6], (BLOCKS, HID), 0.5, 3.0, ((0, 128),), jnp.float32)
    second_weight = noise(keys[7], (BLOCKS, HID, HID), HID ** -0.5, 0.375, ((0, 128),))
    second_bias = noise(keys[8], (BLOCKS, HID), 0.5, 3.0, ((0, 128),), jnp.float32)
    third_weight = noise(keys[9], (BLOCKS, RAW_CH, HID), HID ** -0.5, 0.375, ((0, 128),))
    third_bias = noise(keys[10], (BLOCKS, RAW_CH), 1.0, 4.0, ((0, 128),), jnp.float32)
    return dict(block_ids=block_ids, positions=positions, spacing=spacing, lengths=lengths, color_grad=color_grad, first_weight=first_weight, first_bias=first_bias, second_weight=second_weight, second_bias=second_bias, third_weight=third_weight, third_bias=third_bias)


def encode(points):
    frequency = math.pi * jnp.exp2(jnp.arange(LEVELS, dtype=jnp.float32) * (8.0 / LEVELS))
    angles = (points[:, :, None] * frequency[None, None, :]).reshape(points.shape[0], 3 * LEVELS)
    return jnp.concatenate([jnp.sin(angles), jnp.cos(angles)], axis=1).astype(jnp.bfloat16)

def swish_slope(pre):
    sigmo = jax.nn.sigmoid(pre)
    return sigmo * (1.0 + pre * (1.0 - sigmo))

def forward(features, first_weight, first_bias, second_weight, second_bias, third_weight, third_bias):
    first_pre = jnp.dot(features, first_weight, preferred_element_type=jnp.float32) + first_bias
    first_act = jax.nn.silu(first_pre).astype(jnp.bfloat16)
    second_pre = jnp.dot(first_act, second_weight, preferred_element_type=jnp.float32) + second_bias
    second_act = jax.nn.silu(second_pre).astype(jnp.bfloat16)
    field_out = jnp.dot(second_act, third_weight.T, preferred_element_type=jnp.float32) + third_bias
    return (first_pre, first_act, second_pre, second_act, field_out)

def backward(features, first_pre, first_act, second_pre, second_act, out_grad, second_weight, third_weight):
    highest = lax.Precision.HIGHEST
    second_grad = jnp.dot(out_grad, third_weight.astype(jnp.float32), precision=highest)
    second_delta = (second_grad * swish_slope(second_pre)).astype(jnp.bfloat16)
    first_grad = jnp.dot(second_delta, second_weight.T, preferred_element_type=jnp.float32)
    first_delta = (first_grad * swish_slope(first_pre)).astype(jnp.bfloat16)
    return (jnp.dot(features.T, first_delta, preferred_element_type=jnp.float32), lax.optimization_barrier(jnp.sum(first_delta.astype(jnp.float32), axis=0)), jnp.dot(first_act.T, second_delta, preferred_element_type=jnp.float32), lax.optimization_barrier(jnp.sum(second_delta.astype(jnp.float32), axis=0)), jnp.dot(out_grad.T, second_act.astype(jnp.float32), precision=highest), lax.optimization_barrier(jnp.sum(out_grad, axis=0)))

def render(field_out, spacing, lengths):
    sample_index = jnp.arange(field_out.shape[1], dtype=jnp.int32)
    live_mask = sample_index[None, :] < lengths[:, None]
    density = jax.nn.softplus(field_out[:, :, 0])
    shade = jax.nn.sigmoid(field_out[:, :, 1:])
    depth_step = jnp.where(live_mask, density * spacing, 0.0)
    log_trans = depth_step - jnp.cumsum(depth_step, axis=1)
    weight = jnp.exp(log_trans) * -jnp.expm1(-depth_step)
    return lax.optimization_barrier(jnp.sum(weight[:, :, None] * shade, axis=1)).T

def reference(block_ids, positions, spacing, lengths, color_grad, first_weight, first_bias, second_weight, second_bias, third_weight, third_bias):
    flat_ids = block_ids.reshape(-1).astype(jnp.int32)
    total = flat_ids.shape[0]
    points = positions.reshape(3, total).T
    group_cap = N_GRP * N_CELL * CAP
    sorter = jnp.argsort(flat_ids, stable=True).astype(jnp.int32)
    sorted_ids = flat_ids[sorter]
    block_range = jnp.arange(BLOCKS, dtype=jnp.int32)
    starts = jnp.searchsorted(sorted_ids, block_range, side='left').astype(jnp.int32)
    ends = jnp.searchsorted(sorted_ids, block_range, side='right').astype(jnp.int32)
    rank_in = jnp.arange(total, dtype=jnp.int32) - starts[sorted_ids]
    slot_index = jnp.zeros((total,), jnp.int32).at[sorter].set(sorted_ids * group_cap + rank_in)
    offsets = jnp.arange(group_cap, dtype=jnp.int32)

    def members(block_index):
        picks = jnp.clip(starts[block_index] + offsets, 0, total - 1).astype(jnp.int32)
        return (sorter[picks], offsets < ends[block_index] - starts[block_index])

    def forward_block(block_index):
        rows_here, live_rows = members(block_index)
        features = encode(points[rows_here])
        return forward(features, first_weight[block_index], first_bias[block_index], second_weight[block_index], second_bias[block_index], third_weight[block_index], third_bias[block_index])[4]
    outputs_all = lax.map(forward_block, block_range)
    field_out = outputs_all.reshape(-1, RAW_CH)[slot_index].reshape(spacing.shape[0], spacing.shape[1], RAW_CH)
    color, pullback = jax.vjp(lambda values: render(values, spacing, lengths), field_out)
    out_grad = pullback(color_grad)[0].reshape(total, RAW_CH)

    def backward_block(block_index):
        rows_here, live_rows = members(block_index)
        features = encode(points[rows_here])
        first_pre, first_act, second_pre, second_act, unused = forward(features, first_weight[block_index], first_bias[block_index], second_weight[block_index], second_bias[block_index], third_weight[block_index], third_bias[block_index])
        sample_grad = jnp.where(live_rows[:, None], out_grad[rows_here], 0.0)
        return backward(features, first_pre, first_act, second_pre, second_act, sample_grad, second_weight[block_index], third_weight[block_index])
    grads = lax.map(backward_block, block_range)
    return (grads[0], grads[1], grads[2], grads[3], grads[4], grads[5])
```

```python
import functools
import math

import jax
import jax.numpy as jnp
from jax import lax
from jax.experimental import pallas as pl
from jax.experimental.pallas import tpu as pltpu
from jax.sharding import PartitionSpec as P

MESH = pl.DeviceIdType.MESH
F32 = jnp.float32
BF16 = jnp.bfloat16

CHANNELS = 4
RANKS = 8
LEVELS = 16
SINE = (6.283164044295505, -41.33714237020527, 81.34076885897593, -70.99343300945087)

NN = (((1,), (0,)), ((), ()))
NT = (((1,), (1,)), ((), ()))


def matmul(a, b, dims=NN):
    return lax.dot_general(a, b, dims, preferred_element_type=F32)


def turns_cosine(turns):
    rest = turns - jnp.round(turns)
    w = 0.25 - jnp.abs(rest)
    square = w * w
    poly = SINE[3]
    for coefficient in SINE[2::-1]:
        poly = poly * square + coefficient
    return w * poly


def split(values, parts):
    pieces = []
    for _ in range(parts - 1):
        piece = values.astype(BF16).astype(F32)
        pieces.append(piece)
        values = values - piece
    pieces.append(values)
    return pieces


def column(row):
    n = row.shape[1]
    diagonal = lax.broadcasted_iota(jnp.int32, (n, n), 0) == lax.broadcasted_iota(
        jnp.int32, (n, n), 1
    )
    return jnp.sum(jnp.where(diagonal, jnp.broadcast_to(row, (n, n)), 0.0), axis=1, keepdims=True)


def kernel(
    sizes,
    ids_ref,
    positions_ref,
    spacing_ref,
    lengths_ref,
    color_grad_ref,
    w1_ref,
    b1_ref,
    w2_ref,
    b2_ref,
    w3_ref,
    b3_ref,
    g1_out,
    g2_out,
    gs_out,
    v8,
    av,
    bt2,
    packed,
    bsend1,
    brecv1,
    asend1,
    arecv1,
    asend2,
    arecv2,
    bsend2,
    brecv2,
    bsend3,
    brecv3,
    asend3,
    arecv3,
    feat,
    act1,
    act2,
    slope1,
    slope2,
    delta1,
    delta2,
    og16,
    w1_own,
    w2_own,
    w1t,
    w2t,
    w3t,
    b2_wide,
    g1_own,
    g2_own,
    gs_own,
    load_sem,
    send_sem,
    recv_sem,
    own_sem,
):
    copies, group, levels_z, rays, samples = sizes
    inner = group // copies
    lanes = 2 * samples
    rows = rays // 2
    total = rays * samples
    width = levels_z * RANKS
    height = group * CHANNELS
    slots = group * width
    hidden = w2_own.shape[0]
    enc = w1_own.shape[0]

    y = lax.axis_index("grp")
    cell = lax.axis_index("cell")
    z = cell // inner
    inside = cell % inner
    me = y * inner + inside

    def device_a(peer):
        return {"grp": peer // inner, "cell": z * inner + peer % inner}

    def device_b(peer):
        return {"grp": y, "cell": peer * inner + inside}

    load1 = pltpu.make_async_copy(w1_ref.at[y], w1_own, load_sem.at[0])
    load2 = pltpu.make_async_copy(w2_ref.at[y], w2_own, load_sem.at[1])
    load1.start()
    load2.start()

    barrier = pltpu.get_barrier_semaphore()

    def greet_a(k, carry):
        pl.semaphore_signal(
            barrier, inc=1, device_id=device_a((me + k) % group), device_id_type=MESH
        )
        return carry

    def greet_b(k, carry):
        pl.semaphore_signal(
            barrier, inc=1, device_id=device_b((z + k) % levels_z), device_id_type=MESH
        )
        return carry

    lax.fori_loop(1, group, greet_a, 0)
    lax.fori_loop(1, levels_z, greet_b, 0)

    def exchange(source, target, index, own, count, device):
        target[own] = source[own]

        def send(k, carry):
            peer = (own + k) % count
            pltpu.make_async_remote_copy(
                src_ref=source.at[peer],
                dst_ref=target.at[own],
                send_sem=send_sem.at[index],
                recv_sem=recv_sem.at[index],
                device_id=device(peer),
                device_id_type=MESH,
            ).start()
            return carry

        lax.fori_loop(1, count, send, 0)
        others = target.at[pl.ds(0, count - 1)]
        pltpu.make_async_copy(others, others, recv_sem.at[index]).wait()

    def sent(source, index, count):
        others = source.at[pl.ds(0, count - 1)]
        pltpu.make_async_copy(others, others, send_sem.at[index]).wait()

    def exchange_a(source, target, index):
        exchange(source, target, index, me, group, device_a)

    def exchange_b(source, target, index):
        exchange(source, target, index, z, levels_z, device_b)

    def pair(values):
        return jnp.concatenate([values[:rows], values[rows:]], axis=1)

    ids = pair(ids_ref[...])
    ids_f = ids.astype(F32)
    square = ids_f
    if rows < lanes:
        square = jnp.concatenate([ids_f, jnp.full((lanes - rows, lanes), -1.0, F32)], axis=0)
    columns = square.T
    earlier = lax.broadcasted_iota(jnp.int32, (lanes, lanes), 0) < lax.broadcasted_iota(
        jnp.int32, (lanes, lanes), 1
    )
    id_rows = [ids_f[g : g + 1] for g in range(rows)]
    counts = [jnp.zeros((8, lanes), F32) for _ in range(rows)]
    for first in range(rows):
        wide = jnp.broadcast_to(columns[:, first : first + 1], (lanes, lanes))
        for g in range(first, rows):
            same = wide == id_rows[g]
            if g == first:
                same = same & earlier
            hits = jnp.where(same, 1.0, 0.0)
            counts[g] = counts[g] + jnp.sum(hits.reshape(lanes // 8, 8, lanes), axis=0)
    owner = ids // copies
    key_a = (ids % copies) * inner + owner % inner
    key_b = (owner // inner) * RANKS
    keys_a = [key_a[g : g + 1] for g in range(rows)]
    slot_row = lax.broadcasted_iota(jnp.int32, (width, lanes), 0)
    owner_row = lax.broadcasted_iota(jnp.int32, (height, lanes), 0) // CHANNELS
    for g in range(rows):
        rank = jnp.sum(counts[g], axis=0, keepdims=True).astype(jnp.int32)
        hit = jnp.where(slot_row == key_b[g : g + 1] + rank, 1.0, 0.0).astype(BF16)
        bt2[0:width, g * lanes : (g + 1) * lanes] = hit
        bt2[width : 2 * width, g * lanes : (g + 1) * lanes] = hit

    def spread(channels, parts):
        for c in range(CHANNELS):
            values = channels[c]
            v8[:, c, :] = values
            v8[:, c + CHANNELS, :] = values
        for g in range(rows):
            mine = owner_row == keys_a[g]
            for p, piece in enumerate(split(v8[g], parts)):
                tall = jnp.concatenate([piece] * (height // 8), axis=0)
                av[p * height : (p + 1) * height, g * lanes : (g + 1) * lanes] = jnp.where(
                    mine, tall, 0.0
                ).astype(BF16)
        wide = matmul(bt2[0:width], av[0 : parts * height], NT)
        result = wide[:, 0:height]
        for p in range(1, parts):
            result = result + wide[:, p * height : (p + 1) * height]
        return result

    def put_b(target, values):
        target[...] = values.reshape(levels_z, RANKS, height)

    def put_a(target, values):
        for j in range(group):
            target[j] = values[j * CHANNELS : (j + 1) * CHANNELS]

    def get_a(source):
        return jnp.concatenate([source[j] for j in range(group)], axis=0)

    positions = [pair(positions_ref[k]) for k in range(3)]
    put_b(bsend1, spread(positions + [jnp.zeros((rows, lanes), F32)], 3))

    pl.semaphore_wait(barrier, group - 1 + levels_z - 1)

    exchange_b(bsend1, brecv1, 0)
    put_a(asend1, brecv1[...].reshape(width, height).T)

    load1.wait()
    load2.wait()
    tall = feat.shape[0]
    b1 = b1_ref[pl.ds(y, 1), :]
    bias_rows = [piece for piece in split(b1, 3)]
    w1_all = jnp.concatenate(
        [w1_own[...].astype(F32)] + bias_rows + [jnp.zeros((tall - enc - 3, hidden), F32)], axis=0
    )
    w1t[...] = (w1_all * 0.5).T.astype(BF16)
    w2t[...] = (w2_own[...].astype(F32) * 0.5).T.astype(BF16)
    w3 = w3_ref[y].astype(F32)
    w3_tall = jnp.concatenate([w3, w3, jnp.zeros((lanes - 2 * CHANNELS, hidden), F32)], axis=0)
    w3t[...] = w3_tall.T[:, 0 : 4 * CHANNELS].astype(BF16)
    w3_rows = jnp.concatenate([w3, jnp.zeros((3 * CHANNELS, hidden), F32)], axis=0).astype(BF16)
    b2_wide[...] = jnp.broadcast_to(b2_ref[pl.ds(y, 1), :] * 0.5, (lanes, hidden)).T
    b3 = column(b3_ref[pl.ds(y, 1), :])
    one_row = lax.broadcasted_iota(jnp.int32, (tall - enc, slots), 0) < 3
    feat[enc:tall, :] = jnp.where(one_row, 1.0, 0.0).astype(BF16)
    act1[hidden:, :] = jnp.ones((act1.shape[0] - hidden, slots), BF16)

    exchange_a(asend1, arecv1, 1)

    level = lax.broadcasted_iota(jnp.int32, (3 * LEVELS, width), 0) % LEVELS
    half_turns = jnp.left_shift(1, level // 2).astype(F32) * jnp.where(
        level % 2 == 1, 0.5 * math.sqrt(2.0), 0.5
    )
    per_step = 4
    step_lanes = per_step * width

    def encode_step(j, carry):
        at = pl.ds(pl.multiple_of(j * width, width), width)
        point = arecv1[j]
        tall_point = jnp.concatenate(
            [jnp.broadcast_to(point[k : k + 1], (LEVELS, width)) for k in range(3)], axis=0
        )
        turns = tall_point * half_turns
        feat[0 : 3 * LEVELS, at] = turns_cosine(turns - 0.25).astype(BF16)
        feat[3 * LEVELS : 6 * LEVELS, at] = turns_cosine(turns).astype(BF16)
        return carry

    def activate(half, act, slope, at):
        bent = jnp.tanh(half)
        product = half * bent
        active = (half + product).astype(BF16)
        act[0:hidden, at] = active
        slope[:, at] = ((half + 1.0) - product) * (0.5 * bent + 0.5)
        return active

    def forward_step(i, carry):
        at = pl.ds(pl.multiple_of(i * step_lanes, step_lanes), step_lanes)
        first = activate(matmul(w1t[...], feat[:, at]), act1, slope1, at)
        bias = jnp.concatenate([b2_wide[...]] * (step_lanes // lanes), axis=1)
        second = activate(matmul(w2t[...], first) + bias, act2, slope2, at)
        out = matmul(w3_rows, second)[0:CHANNELS] + b3
        for k in range(per_step):
            asend2[i * per_step + k] = out[:, k * width : (k + 1) * width]
        return carry

    lax.fori_loop(0, group, encode_step, 0)
    lax.fori_loop(0, group // per_step, forward_step, 0)

    exchange_a(asend2, arecv2, 2)
    put_b(bsend2, get_a(arecv2).T)
    exchange_b(bsend2, brecv2, 3)
    returned = jnp.concatenate(split(brecv2[...].reshape(width, height).T, 2), axis=1).astype(BF16)
    for g in range(rows):
        at = slice(g * lanes, (g + 1) * lanes)
        found = matmul(returned, bt2[:, at])
        kept = jnp.where(owner_row == keys_a[g], found, 0.0)
        both = jnp.sum(kept.reshape(height // 8, 8, lanes), axis=0)
        v8[g] = both
    field = [v8[:, c, :] + v8[:, c + CHANNELS, :] for c in range(CHANNELS)]

    lane = lax.broadcasted_iota(jnp.int32, (rows, lanes), 1)
    left = lane < samples

    def per_ray(row):
        tall_row = column(row)
        return jnp.where(left, tall_row[:rows], tall_row[rows:])

    lengths = per_ray(lengths_ref[...].astype(F32))
    tint = [per_ray(color_grad_ref[c : c + 1, :]) for c in range(3)]
    spacing = pair(spacing_ref[...])
    before = lax.broadcasted_iota(jnp.int32, (lanes, lanes), 0)
    after = lax.broadcasted_iota(jnp.int32, (lanes, lanes), 1)
    same_ray = (before // samples) == (after // samples)

    def scan(values, mask):
        ones = jnp.where(mask & same_ray, 1.0, 0.0).astype(BF16)
        pieces = jnp.concatenate(split(values, 3), axis=0).astype(BF16)
        sums = matmul(pieces, ones)
        return sums[0:rows] + sums[rows : 2 * rows] + sums[2 * rows : 3 * rows]

    live = (lane % samples).astype(F32) < lengths
    density = jnp.maximum(field[0], 0.0) + jnp.log1p(jnp.exp(-jnp.abs(field[0])))
    step = jnp.where(live, density * spacing, 0.0)
    left_over = jnp.exp(-step)
    series = step * (
        1.0 - step * (1 / 2) * (1.0 - step * (1 / 3) * (1.0 - step * (1 / 4) * (1.0 - step * (1 / 5))))
    )
    absorbed = jnp.where(step < 0.05, series, 1.0 - left_over)
    trans = jnp.exp(-scan(step, before < after))
    weight = trans * absorbed
    shade = [0.5 + 0.5 * jnp.tanh(0.5 * field[c]) for c in range(1, CHANNELS)]
    seen = tint[0] * shade[0] + tint[1] * shade[1] + tint[2] * shade[2]
    behind = scan(weight * seen, before > after)
    step_grad = trans * left_over * seen - behind
    density_slope = 0.5 + 0.5 * jnp.tanh(0.5 * field[0])
    out_grad = [jnp.where(live, step_grad * spacing * density_slope, 0.0)]
    for c in range(3):
        out_grad.append(weight * tint[c] * shade[c] * (1.0 - shade[c]))

    put_b(bsend3, spread(out_grad, 2))
    exchange_b(bsend3, brecv3, 4)
    put_a(asend3, brecv3[...].reshape(width, height).T)
    exchange_a(asend3, arecv3, 5)

    def gather_step(j, carry):
        at = pl.ds(pl.multiple_of(j * width, width), width)
        grad = arecv3[j]
        packed[:, at] = grad
        og16[:, at] = jnp.concatenate(
            split(grad, 2) + [jnp.zeros((2 * CHANNELS, width), F32)], axis=0
        ).astype(BF16)
        return carry

    lax.fori_loop(0, group, gather_step, 0)

    def backward_second(i, carry):
        at = pl.ds(pl.multiple_of(i * step_lanes, step_lanes), step_lanes)
        delta2[:, at] = (matmul(w3t[...], og16[:, at]) * slope2[:, at]).astype(BF16)
        return carry

    lax.fori_loop(0, group // per_step, backward_second, 0)
    second = matmul(act1[...], delta2[...], NT)
    g2_own[...] = second[0:hidden].astype(BF16)

    def share(own, out, index):
        pltpu.make_async_copy(own, out.at[y], own_sem.at[index]).start()

        def send(k, carry):
            pltpu.make_async_remote_copy(
                src_ref=own,
                dst_ref=out.at[y],
                send_sem=send_sem.at[6 + index],
                recv_sem=recv_sem.at[6 + index],
                device_id={"grp": (y + k) % copies, "cell": cell},
                device_id_type=MESH,
            ).start()
            return carry

        lax.fori_loop(1, copies, send, 0)

    share(g2_own, g2_out, 0)

    def backward_first(i, carry):
        at = pl.ds(pl.multiple_of(i * step_lanes, step_lanes), step_lanes)
        delta1[:, at] = (matmul(w2_own[...], delta2[:, at]) * slope1[:, at]).astype(BF16)
        return carry

    lax.fori_loop(0, group // per_step, backward_first, 0)
    first = matmul(feat[...], delta1[...], NT)
    g1_own[...] = first[0:enc].astype(BF16)
    share(g1_own, g1_out, 1)
    third = matmul(og16[...], act2[...], NT)
    third_bias = jnp.sum(packed[...], axis=1, keepdims=True)
    gs_own[...] = jnp.concatenate(
        [
            first[enc : enc + 1],
            second[hidden : hidden + 1],
            jnp.zeros((2, hidden), F32),
            third[0:CHANNELS] + third[CHANNELS : 2 * CHANNELS],
            jnp.broadcast_to(third_bias, (CHANNELS, hidden)),
            jnp.zeros((4, hidden), F32),
        ],
        axis=0,
    )
    share(gs_own, gs_out, 2)

    for own, out, index in ((g2_own, g2_out, 0), (g1_own, g1_out, 1), (gs_own, gs_out, 2)):
        pltpu.make_async_copy(own, out.at[y], own_sem.at[index]).wait()
        others = out.at[pl.ds(0, copies - 1)]
        pltpu.make_async_copy(others, others, recv_sem.at[6 + index]).wait()
        pltpu.make_async_copy(others, others, send_sem.at[6 + index]).wait()
    sent(bsend1, 0, levels_z)
    sent(asend1, 1, group)
    sent(asend2, 2, group)
    sent(bsend2, 3, levels_z)
    sent(bsend3, 4, levels_z)
    sent(asend3, 5, group)


def local(levels_z, copies, *args):
    (ids, positions, spacing, lengths, color_grad, w1, b1, w2, b2, w3, b3) = args
    rays, samples = spacing.shape
    inner = lax.axis_size("cell") // levels_z
    group = copies * inner
    width = levels_z * RANKS
    height = group * CHANNELS
    slots = group * width
    blocks, enc, hidden = w1.shape
    total = rays * samples
    lanes = 2 * samples
    rows = rays // 2
    tall = enc + 16
    vmem = pl.BlockSpec(memory_space=pltpu.VMEM)
    hbm = pl.BlockSpec(memory_space=pl.ANY)
    part_a = pltpu.VMEM((group, CHANNELS, width), F32)
    part_b = pltpu.VMEM((levels_z, RANKS, height), F32)
    flops = 2 * slots * (3 * hidden * hidden + 3 * enc * hidden)
    g1, g2, gs = pl.pallas_call(
        functools.partial(kernel, (copies, group, levels_z, rays, samples)),
        out_shape=[
            jax.ShapeDtypeStruct((blocks, enc, hidden), BF16),
            jax.ShapeDtypeStruct((blocks, hidden, hidden), BF16),
            jax.ShapeDtypeStruct((blocks, 16, hidden), F32),
        ],
        in_specs=[vmem, vmem, vmem, vmem, vmem, hbm, vmem, hbm, vmem, vmem, vmem],
        out_specs=[hbm, hbm, hbm],
        scratch_shapes=[
            pltpu.VMEM((rows, 8, lanes), F32),
            pltpu.VMEM((3 * height, total), BF16),
            pltpu.VMEM((2 * width, total), BF16),
            pltpu.VMEM((CHANNELS, slots), F32),
            part_b,
            part_b,
            part_a,
            part_a,
            part_a,
            part_a,
            part_b,
            part_b,
            part_b,
            part_b,
            part_a,
            part_a,
            pltpu.VMEM((tall, slots), BF16),
            pltpu.VMEM((hidden + 16, slots), BF16),
            pltpu.VMEM((hidden, slots), BF16),
            pltpu.VMEM((hidden, slots), F32),
            pltpu.VMEM((hidden, slots), F32),
            pltpu.VMEM((hidden, slots), BF16),
            pltpu.VMEM((hidden, slots), BF16),
            pltpu.VMEM((4 * CHANNELS, slots), BF16),
            pltpu.VMEM((enc, hidden), BF16),
            pltpu.VMEM((hidden, hidden), BF16),
            pltpu.VMEM((hidden, tall), BF16),
            pltpu.VMEM((hidden, hidden), BF16),
            pltpu.VMEM((hidden, 4 * CHANNELS), BF16),
            pltpu.VMEM((hidden, lanes), F32),
            pltpu.VMEM((enc, hidden), BF16),
            pltpu.VMEM((hidden, hidden), BF16),
            pltpu.VMEM((16, hidden), F32),
            pltpu.SemaphoreType.DMA((2,)),
            pltpu.SemaphoreType.DMA((9,)),
            pltpu.SemaphoreType.DMA((9,)),
            pltpu.SemaphoreType.DMA((3,)),
        ],
        compiler_params=pltpu.CompilerParams(
            collective_id=0, has_side_effects=True, vmem_limit_bytes=48 * 1024 * 1024
        ),
        cost_estimate=pl.CostEstimate(flops=flops, bytes_accessed=1 << 21, transcendentals=slots * hidden * 2),
    )(
        ids.reshape(rays, samples),
        positions,
        spacing,
        lengths.reshape(1, rays),
        color_grad,
        w1,
        b1,
        w2,
        b2,
        w3,
        b3,
    )
    return (
        g1.astype(F32),
        gs[:, 0, :],
        g2.astype(F32),
        gs[:, 1, :],
        gs[:, 4:8, :],
        gs[:, 8:12, 0],
    )


def solution(mesh):
    copies, cells = mesh.shape["grp"], mesh.shape["cell"]
    levels_z = 16 if cells % 16 == 0 and cells >= 128 else 2
    in_specs = (
        P(("grp", "cell"), None, None),
        P(None, ("grp", "cell"), None),
        P(("grp", "cell"), None),
        P(("grp", "cell")),
        P(None, ("grp", "cell")),
        P("cell", None, None),
        P("cell", None),
        P("cell", None, None),
        P("cell", None),
        P("cell", None, None),
        P("cell", None),
    )
    out_specs = (
        P("cell", None, None),
        P("cell", None),
        P("cell", None, None),
        P("cell", None),
        P("cell", None, None),
        P("cell", None),
    )
    return jax.shard_map(
        functools.partial(local, levels_z, copies),
        mesh=mesh,
        in_specs=in_specs,
        out_specs=out_specs,
        check_vma=False,
    )
```

```python
import functools
import math

import jax
import jax.numpy as jnp
from jax import lax
from jax.experimental import pallas as pl
from jax.experimental.pallas import tpu as pltpu
from jax.sharding import PartitionSpec as P

MESH = pl.DeviceIdType.MESH
F32 = jnp.float32
BF16 = jnp.bfloat16

CHANNELS = 4
RANKS = 8
LEVELS = 16
VMEM_BYTES = 64 * 1024 * 1024 - 64 * 1024
SINE = (6.283164044295505, -41.33714237020527, 81.34076885897593, -70.99343300945087)

NN = (((1,), (0,)), ((), ()))
NT = (((1,), (1,)), ((), ()))


def matmul(a, b, dims=NN):
    return lax.dot_general(a, b, dims, preferred_element_type=F32)


def turns_cosine(turns):
    rest = turns - jnp.round(turns)
    w = 0.25 - jnp.abs(rest)
    square = w * w
    poly = SINE[3]
    for coefficient in SINE[2::-1]:
        poly = poly * square + coefficient
    return w * poly


def split(values, parts):
    pieces = []
    for _ in range(parts - 1):
        piece = values.astype(BF16).astype(F32)
        pieces.append(piece)
        values = values - piece
    pieces.append(values)
    return pieces


def column(row):
    n = row.shape[1]
    diagonal = lax.broadcasted_iota(jnp.int32, (n, n), 0) == lax.broadcasted_iota(
        jnp.int32, (n, n), 1
    )
    return jnp.sum(jnp.where(diagonal, jnp.broadcast_to(row, (n, n)), 0.0), axis=1, keepdims=True)


def swap(tiles):
    lanes = tiles.shape[2]
    part = lanes // 8
    sub = lax.broadcasted_iota(jnp.int32, tiles.shape, 1)
    lane = lax.broadcasted_iota(jnp.int32, tiles.shape, 2) // part
    for bit in (1, 2, 4):
        low = pltpu.roll(pltpu.roll(tiles, 8 - bit, 1), bit * part, 2)
        high = pltpu.roll(pltpu.roll(tiles, bit, 1), lanes - bit * part, 2)
        sub_set = (sub & bit) != 0
        lane_set = (lane & bit) != 0
        moved = jnp.where(lane_set, low, high)
        tiles = jnp.where(sub_set == lane_set, tiles, moved)
    return tiles


def kernel(
    sizes,
    ids_hbm,
    positions_hbm,
    spacing_hbm,
    lengths_hbm,
    color_grad_hbm,
    w1_hbm,
    b1_hbm,
    w2_hbm,
    b2_hbm,
    w3_hbm,
    b3_hbm,
    g1_out,
    g2_out,
    gs_out,
    ids_ref,
    positions_ref,
    spacing_ref,
    lengths_ref,
    color_grad_ref,
    b1_ref,
    b2_ref,
    w3_ref,
    b3_ref,
    v8,
    av,
    bt2,
    asend1,
    arecv1,
    bsend1,
    brecv1,
    bsend2,
    brecv2,
    asend2,
    arecv2,
    asend3,
    arecv3,
    bsend3,
    brecv3,
    feat,
    act1,
    act2,
    slope1,
    slope2,
    delta1,
    delta2,
    og16,
    og_sum,
    second_sum,
    w1_own,
    w2_own,
    w1t,
    w2t,
    w3t,
    b2_wide,
    g1_own,
    g2_own,
    gs_own,
    load_sem,
    send_sem,
    recv_sem,
    near_sem,
    own_sem,
):
    copies, group, levels_z, rays, samples = sizes
    inner = group // copies
    lanes = 2 * samples
    rows = rays // 2
    total = rays * samples
    width = levels_z * RANKS
    height = group * CHANNELS
    slots = group * width
    hidden = w2_own.shape[0]
    enc = w1_own.shape[0]

    y = lax.axis_index("grp")
    cell = lax.axis_index("cell")
    z = cell // inner
    inside = cell % inner
    me = y * inner + inside

    def device_a(peer):
        return {"grp": peer // inner, "cell": z * inner + peer % inner}

    def device_b(peer):
        return {"grp": y, "cell": peer * inner + inside}

    barrier = pltpu.get_barrier_semaphore()

    def greet_a(k, carry):
        pl.semaphore_signal(
            barrier, inc=1, device_id=device_a((me + k) % group), device_id_type=MESH
        )
        return carry

    def far_first(k):
        left = levels_z - k
        odd = left % 2
        return (z + odd * ((left + 1) // 2) + (1 - odd) * (levels_z - left // 2)) % levels_z

    def greet_b(k, carry):
        pl.semaphore_signal(barrier, inc=1, device_id=device_b(far_first(k)), device_id_type=MESH)
        return carry

    lax.fori_loop(1, levels_z, greet_b, 0)
    lax.fori_loop(1, group, greet_a, 0)

    loads = [
        pltpu.make_async_copy(source, target, load_sem.at[i])
        for i, (source, target) in enumerate(
            (
                (ids_hbm, ids_ref),
                (positions_hbm, positions_ref),
                (w2_hbm.at[y], w2_own),
                (w1_hbm.at[y], w1_own),
                (b1_hbm, b1_ref),
                (b2_hbm, b2_ref),
                (w3_hbm, w3_ref),
                (b3_hbm, b3_ref),
                (spacing_hbm, spacing_ref),
                (lengths_hbm, lengths_ref),
                (color_grad_hbm, color_grad_ref),
            )
        )
    ]
    for load in loads:
        load.start()
    loads[0].wait()

    def send(source, target, index, own, peer, device, arrived):
        pltpu.make_async_remote_copy(
            src_ref=source.at[peer],
            dst_ref=target.at[own],
            send_sem=send_sem.at[index],
            recv_sem=arrived,
            device_id=device,
            device_id_type=MESH,
        ).start()

    def wait_all(buffer, count, sem):
        others = buffer.at[pl.ds(0, count - 1)]
        pltpu.make_async_copy(others, others, sem).wait()

    def exchange_a(source, target, index):
        target[me] = source[me]

        def step(k, carry):
            peer = (me + k) % group
            send(source, target, index, me, peer, device_a(peer), recv_sem.at[index])
            return carry

        lax.fori_loop(1, group, step, 0)
        wait_all(target, group, recv_sem.at[index])

    def send_b(source, target, index, row):
        target[z] = source[z]

        def step(k, carry):
            peer = far_first(k)
            send(source, target, index, z, peer, device_b(peer), near_sem.at[row, z])
            return carry

        lax.fori_loop(1, levels_z, step, 0)

    def arrival(target, row, peer):
        pltpu.make_async_copy(target.at[peer], target.at[peer], near_sem.at[row, peer]).wait()

    def pair(values):
        return jnp.concatenate([values[:rows], values[rows:]], axis=1)

    ids = pair(ids_ref[...])
    ids_f = ids.astype(F32)
    square = ids_f
    if rows < lanes:
        square = jnp.concatenate([ids_f, jnp.full((lanes - rows, lanes), -1.0, F32)], axis=0)
    columns = square.T
    earlier = lax.broadcasted_iota(jnp.int32, (lanes, lanes), 0) < lax.broadcasted_iota(
        jnp.int32, (lanes, lanes), 1
    )
    id_rows = [ids_f[g : g + 1] for g in range(rows)]
    counts = [jnp.zeros((8, lanes), F32) for _ in range(rows)]
    for first in range(rows):
        wide = jnp.broadcast_to(columns[:, first : first + 1], (lanes, lanes))
        for g in range(first, rows):
            same = wide == id_rows[g]
            if g == first:
                same = same & earlier
            hits = jnp.where(same, 1.0, 0.0)
            counts[g] = counts[g] + jnp.sum(hits.reshape(lanes // 8, 8, lanes), axis=0)
    owner = ids // copies
    key_a = (ids % copies) * inner + owner % inner
    key_b = (owner // inner) * RANKS
    keys_a = [key_a[g : g + 1] for g in range(rows)]
    slot_row = lax.broadcasted_iota(jnp.int32, (width, lanes), 0)
    owner_row = lax.broadcasted_iota(jnp.int32, (height, lanes), 0) // CHANNELS
    for g in range(rows):
        rank = jnp.sum(counts[g], axis=0, keepdims=True).astype(jnp.int32)
        hit = jnp.where(slot_row == key_b[g : g + 1] + rank, 1.0, 0.0).astype(BF16)
        bt2[0:width, g * lanes : (g + 1) * lanes] = hit
        bt2[width : 2 * width, g * lanes : (g + 1) * lanes] = hit

    def spread(channels, parts):
        for c in range(CHANNELS):
            values = channels[c]
            v8[:, c, :] = values
            v8[:, c + CHANNELS, :] = values
        for g in range(rows):
            mine = owner_row == keys_a[g]
            for p, piece in enumerate(split(v8[g], parts)):
                tall = jnp.concatenate([piece] * (height // 8), axis=0)
                av[p * height : (p + 1) * height, g * lanes : (g + 1) * lanes] = jnp.where(
                    mine, tall, 0.0
                ).astype(BF16)
        wide = matmul(av[0 : parts * height], bt2[0:width], NT)
        result = wide[0:height]
        for p in range(1, parts):
            result = result + wide[p * height : (p + 1) * height]
        return result

    half = group // 2

    def put_a(target, values):
        for j in range(group):
            target[j] = values[j * CHANNELS : (j + 1) * CHANNELS]

    def get_a(source):
        return jnp.concatenate([source[j] for j in range(group)], axis=0)

    def a_to_b(arrived, target):
        tall = jnp.concatenate(
            [
                arrived[h * half : (h + 1) * half, c, :]
                for h in range(2)
                for c in range(CHANNELS)
            ],
            axis=0,
        )
        target[...] = swap(tall.T.reshape(levels_z, RANKS, height))

    def b_to_a(arrived, target):
        tall = swap(arrived[...]).reshape(width, height).T
        for h in range(2):
            for c in range(CHANNELS):
                at = (h * CHANNELS + c) * half
                target[h * half : (h + 1) * half, c, :] = tall[at : at + half]

    loads[1].wait()
    positions = [pair(positions_ref[k]) for k in range(3)]
    put_a(asend1, spread(positions + [jnp.zeros((rows, lanes), F32)], 3))

    for load in loads[2:]:
        load.wait()
    tall = feat.shape[0]
    b1 = b1_ref[pl.ds(y, 1), :]
    bias_rows = [piece for piece in split(b1, 3)]
    w1_all = jnp.concatenate(
        [w1_own[...].astype(F32)] + bias_rows + [jnp.zeros((tall - enc - 3, hidden), F32)], axis=0
    )
    w1t[...] = (w1_all * 0.5).T.astype(BF16)
    w2t[...] = (w2_own[...].astype(F32) * 0.5).T.astype(BF16)
    w3 = w3_ref[y].astype(F32)
    w3_tall = jnp.concatenate([w3, w3, jnp.zeros((lanes - 2 * CHANNELS, hidden), F32)], axis=0)
    w3t[...] = w3_tall.T[:, 0 : 4 * CHANNELS].astype(BF16)
    w3_rows = jnp.concatenate([w3, jnp.zeros((3 * CHANNELS, hidden), F32)], axis=0).astype(BF16)
    b2_wide[...] = jnp.broadcast_to(b2_ref[pl.ds(y, 1), :] * 0.5, (lanes, hidden)).T
    b3 = column(b3_ref[pl.ds(y, 1), :])
    one_row = lax.broadcasted_iota(jnp.int32, (tall - enc, slots), 0) < 3
    feat[enc:tall, :] = jnp.where(one_row, 1.0, 0.0).astype(BF16)
    act1[hidden:, :] = jnp.ones((act1.shape[0] - hidden, slots), BF16)

    second_sum[...] = jnp.zeros(second_sum.shape, F32)
    og_sum[...] = jnp.zeros(og_sum.shape, F32)

    pl.semaphore_wait(barrier, group - 1 + levels_z - 1)
    exchange_a(asend1, arecv1, 0)
    a_to_b(arecv1, bsend1)
    send_b(bsend1, brecv1, 1, 0)

    lane_tile = height
    level = lax.broadcasted_iota(jnp.int32, (3 * LEVELS, lane_tile), 0) % LEVELS
    half_turns = jnp.left_shift(1, level // 2).astype(F32) * jnp.where(
        level % 2 == 1, 0.5 * math.sqrt(2.0), 0.5
    )
    step_lanes = 4 * lane_tile

    def sources(i):
        return (z + levels_z - i) % levels_z, (z + i + 1) % levels_z

    def arrivals(target, row, i):
        first, second = sources(i)

        @pl.when(i > 0)
        def _():
            arrival(target, row, first)

        arrival(target, row, second)
        return first, second

    def encode(point, start):
        for h in range(2):
            at = pl.ds(pl.multiple_of(start + h * lane_tile, lane_tile), lane_tile)
            tall_point = jnp.concatenate(
                [
                    jnp.broadcast_to(
                        point[h * CHANNELS + k : h * CHANNELS + k + 1], (LEVELS, lane_tile)
                    )
                    for k in range(3)
                ],
                axis=0,
            )
            turns = tall_point * half_turns
            feat[0 : 3 * LEVELS, at] = turns_cosine(turns - 0.25).astype(BF16)
            feat[3 * LEVELS : 6 * LEVELS, at] = turns_cosine(turns).astype(BF16)

    def activate(half, act, slope, at):
        bent = jnp.tanh(half)
        product = half * bent
        active = (half + product).astype(BF16)
        act[0:hidden, at] = active
        slope[:, at] = ((half + 1.0) - product) * (0.5 * bent + 0.5)
        return active

    def forward_step(i, carry):
        start = i * step_lanes
        at = pl.ds(pl.multiple_of(start, step_lanes), step_lanes)
        pair_of = arrivals(brecv1, 0, i)
        for s, source in enumerate(pair_of):
            encode(brecv1[source], start + 2 * s * lane_tile)
        first = activate(matmul(w1t[...], feat[:, at]), act1, slope1, at)
        bias = jnp.concatenate([b2_wide[...]] * (step_lanes // lanes), axis=1)
        second = activate(matmul(w2t[...], first) + bias, act2, slope2, at)
        out = matmul(w3_rows, second)[0:CHANNELS] + b3
        for s, source in enumerate(pair_of):
            base = 2 * s * lane_tile
            bsend2[source] = jnp.concatenate(
                [
                    out[:, base : base + lane_tile],
                    out[:, base + lane_tile : base + 2 * lane_tile],
                ],
                axis=0,
            )

        @pl.when(i > 0)
        def _():
            send(bsend2, brecv2, 2, z, pair_of[0], device_b(pair_of[0]), recv_sem.at[2])

        send(bsend2, brecv2, 2, z, pair_of[1], device_b(pair_of[1]), recv_sem.at[2])
        return carry

    lax.fori_loop(0, levels_z // 2, forward_step, 0)

    brecv2[z] = bsend2[z]
    wait_all(brecv2, levels_z, recv_sem.at[2])
    b_to_a(brecv2, asend2)
    exchange_a(asend2, arecv2, 3)
    returned = jnp.concatenate(split(get_a(arecv2), 2), axis=1).astype(BF16)
    for g in range(rows):
        at = slice(g * lanes, (g + 1) * lanes)
        found = matmul(returned, bt2[:, at])
        kept = jnp.where(owner_row == keys_a[g], found, 0.0)
        both = jnp.sum(kept.reshape(height // 8, 8, lanes), axis=0)
        v8[g] = both
    field = [v8[:, c, :] + v8[:, c + CHANNELS, :] for c in range(CHANNELS)]

    lane = lax.broadcasted_iota(jnp.int32, (rows, lanes), 1)
    left = lane < samples

    def per_ray(row):
        tall_row = column(row)
        return jnp.where(left, tall_row[:rows], tall_row[rows:])

    lengths = per_ray(lengths_ref[...].astype(F32))
    tint = [per_ray(color_grad_ref[c : c + 1, :]) for c in range(3)]
    spacing = pair(spacing_ref[...])
    before = lax.broadcasted_iota(jnp.int32, (lanes, lanes), 0)
    after = lax.broadcasted_iota(jnp.int32, (lanes, lanes), 1)
    same_ray = (before // samples) == (after // samples)

    def scan(values, mask):
        ones = jnp.where(mask & same_ray, 1.0, 0.0).astype(BF16)
        pieces = jnp.concatenate(split(values, 3), axis=0).astype(BF16)
        sums = matmul(pieces, ones)
        return sums[0:rows] + sums[rows : 2 * rows] + sums[2 * rows : 3 * rows]

    live = (lane % samples).astype(F32) < lengths
    density = jnp.maximum(field[0], 0.0) + jnp.log1p(jnp.exp(-jnp.abs(field[0])))
    step = jnp.where(live, density * spacing, 0.0)
    left_over = jnp.exp(-step)
    series = step * (
        1.0 - step * (1 / 2) * (1.0 - step * (1 / 3) * (1.0 - step * (1 / 4) * (1.0 - step * (1 / 5))))
    )
    absorbed = jnp.where(step < 0.05, series, 1.0 - left_over)
    trans = jnp.exp(-scan(step, before < after))
    weight = trans * absorbed
    shade = [0.5 + 0.5 * jnp.tanh(0.5 * field[c]) for c in range(1, CHANNELS)]
    seen = tint[0] * shade[0] + tint[1] * shade[1] + tint[2] * shade[2]
    behind = scan(weight * seen, before > after)
    step_grad = trans * left_over * seen - behind
    density_slope = 0.5 + 0.5 * jnp.tanh(0.5 * field[0])
    out_grad = [jnp.where(live, step_grad * spacing * density_slope, 0.0)]
    for c in range(3):
        out_grad.append(weight * tint[c] * shade[c] * (1.0 - shade[c]))

    put_a(asend3, spread(out_grad, 2))
    exchange_a(asend3, arecv3, 4)
    a_to_b(arecv3, bsend3)
    send_b(bsend3, brecv3, 5, 1)

    def backward_second(i, carry):
        start = i * step_lanes
        at = pl.ds(pl.multiple_of(start, step_lanes), step_lanes)
        pair_of = arrivals(brecv3, 1, i)
        tiles = [brecv3[source] for source in pair_of]
        og_sum[...] = og_sum[...] + (tiles[0] + tiles[1])
        grad = jnp.concatenate(
            [tile[h * CHANNELS : (h + 1) * CHANNELS] for tile in tiles for h in range(2)], axis=1
        )
        pieces = jnp.concatenate(
            split(grad, 2) + [jnp.zeros((2 * CHANNELS, step_lanes), F32)], axis=0
        ).astype(BF16)
        og16[:, at] = pieces
        delta = (matmul(w3t[...], pieces) * slope2[:, at]).astype(BF16)
        delta2[:, at] = delta
        second_sum[...] = second_sum[...] + matmul(act1[:, at], delta, NT)
        return carry

    lax.fori_loop(0, levels_z // 2, backward_second, 0)
    second = second_sum[...]
    g2_own[...] = second[0:hidden].astype(BF16)

    def share(own, out, index):
        pltpu.make_async_copy(own, out.at[y], own_sem.at[index]).start()

        def send(k, carry):
            pltpu.make_async_remote_copy(
                src_ref=own,
                dst_ref=out.at[y],
                send_sem=send_sem.at[6 + index],
                recv_sem=recv_sem.at[6 + index],
                device_id={"grp": (y + k) % copies, "cell": cell},
                device_id_type=MESH,
            ).start()
            return carry

        lax.fori_loop(1, copies, send, 0)

    share(g2_own, g2_out, 0)

    def backward_first(i, carry):
        at = pl.ds(pl.multiple_of(i * step_lanes, step_lanes), step_lanes)
        delta1[:, at] = (matmul(w2_own[...], delta2[:, at]) * slope1[:, at]).astype(BF16)
        return carry

    lax.fori_loop(0, levels_z // 2, backward_first, 0)
    first = matmul(feat[...], delta1[...], NT)
    g1_own[...] = first[0:enc].astype(BF16)
    share(g1_own, g1_out, 1)
    third = matmul(og16[...], act2[...], NT)
    og_total = jnp.sum(og_sum[...], axis=1, keepdims=True)
    og_total = og_total[0:CHANNELS] + og_total[CHANNELS : 2 * CHANNELS]
    diagonal = lax.broadcasted_iota(jnp.int32, (CHANNELS, hidden), 0) == lax.broadcasted_iota(
        jnp.int32, (CHANNELS, hidden), 1
    )
    third_bias = jnp.sum(
        jnp.where(diagonal, jnp.broadcast_to(og_total, (CHANNELS, hidden)), 0.0),
        axis=0,
        keepdims=True,
    )
    gs_own[...] = jnp.concatenate(
        [
            first[enc : enc + 1],
            second[hidden : hidden + 1],
            jnp.zeros((2, hidden), F32),
            third[0:CHANNELS] + third[CHANNELS : 2 * CHANNELS],
            third_bias,
            jnp.zeros((7, hidden), F32),
        ],
        axis=0,
    )
    share(gs_own, gs_out, 2)

    for own, out, index in ((g2_own, g2_out, 0), (g1_own, g1_out, 1), (gs_own, gs_out, 2)):
        pltpu.make_async_copy(own, out.at[y], own_sem.at[index]).wait()
        wait_all(out, copies, recv_sem.at[6 + index])
        wait_all(out, copies, send_sem.at[6 + index])
    wait_all(asend1, group, send_sem.at[0])
    wait_all(bsend1, levels_z, send_sem.at[1])
    wait_all(bsend2, levels_z, send_sem.at[2])
    wait_all(asend2, group, send_sem.at[3])
    wait_all(asend3, group, send_sem.at[4])
    wait_all(bsend3, levels_z, send_sem.at[5])


def finish(
    g1, g2, gs, g1_out, b1_out, g2_out, b2_out, g3_out, b3_out,
    g1_b, g2_b, gs_b, g1_f, b1_f, g2_f, b2_f, g3_f, b3_f, load_sems, sems
):
    copies = []

    def put(source, target):
        copy = pltpu.make_async_copy(source, target, sems.at[len(copies)])
        copy.start()
        copies.append(copy)

    blocks = g1.shape[0]
    loads = [pltpu.make_async_copy(gs, gs_b, load_sems.at[2 * blocks])]
    for b in range(blocks):
        loads.append(pltpu.make_async_copy(g2.at[b], g2_b.at[b], load_sems.at[2 * b]))
        loads.append(pltpu.make_async_copy(g1.at[b], g1_b.at[b], load_sems.at[2 * b + 1]))
    for load in loads:
        load.start()
    loads[0].wait()
    for b in range(blocks):
        b1_f[b : b + 1, :] = gs_b[b, 0:1, :]
        b2_f[b : b + 1, :] = gs_b[b, 1:2, :]
        g3_f[b] = gs_b[b, 4:8, :]
        b3_f[b : b + 1, :] = gs_b[b, 8:9, 0 : b3_f.shape[1]]
    put(b1_f, b1_out)
    put(b2_f, b2_out)
    put(g3_f, g3_out)
    put(b3_f, b3_out)
    for b in range(blocks):
        loads[1 + 2 * b].wait()
        g2_f[b] = g2_b[b].astype(F32)
        put(g2_f.at[b], g2_out.at[b])
        loads[2 + 2 * b].wait()
        g1_f[b] = g1_b[b].astype(F32)
        put(g1_f.at[b], g1_out.at[b])
    for copy in copies:
        copy.wait()


def local(levels_z, copies, *args):
    (ids, positions, spacing, lengths, color_grad, w1, b1, w2, b2, w3, b3) = args
    rays, samples = spacing.shape
    inner = lax.axis_size("cell") // levels_z
    group = copies * inner
    width = levels_z * RANKS
    height = group * CHANNELS
    slots = group * width
    blocks, enc, hidden = w1.shape
    total = rays * samples
    lanes = 2 * samples
    rows = rays // 2
    tall = enc + 16
    hbm = pl.BlockSpec(memory_space=pltpu.HBM)
    part_a = pltpu.VMEM((group, CHANNELS, width), F32)
    part_b = pltpu.VMEM((levels_z, RANKS, height), F32)
    flops = 2 * slots * (3 * hidden * hidden + 3 * enc * hidden)
    g1, g2, gs = pl.pallas_call(
        functools.partial(kernel, (copies, group, levels_z, rays, samples)),
        out_shape=[
            jax.ShapeDtypeStruct((blocks, enc, hidden), BF16),
            jax.ShapeDtypeStruct((blocks, hidden, hidden), BF16),
            jax.ShapeDtypeStruct((blocks, 16, hidden), F32),
        ],
        in_specs=[hbm] * 11,
        out_specs=[hbm] * 3,
        scratch_shapes=[
            pltpu.VMEM((rays, samples), jnp.int32),
            pltpu.VMEM((3, rays, samples), F32),
            pltpu.VMEM((rays, samples), F32),
            pltpu.VMEM((1, rays), jnp.int32),
            pltpu.VMEM((3, rays), F32),
            pltpu.VMEM(b1.shape, F32),
            pltpu.VMEM(b2.shape, F32),
            pltpu.VMEM(w3.shape, BF16),
            pltpu.VMEM(b3.shape, F32),
            pltpu.VMEM((rows, 8, lanes), F32),
            pltpu.VMEM((3 * height, total), BF16),
            pltpu.VMEM((2 * width, total), BF16),
            part_a,
            part_a,
            part_b,
            part_b,
            part_b,
            part_b,
            part_a,
            part_a,
            part_a,
            part_a,
            part_b,
            part_b,
            pltpu.VMEM((tall, slots), BF16),
            pltpu.VMEM((hidden + 16, slots), BF16),
            pltpu.VMEM((hidden, slots), BF16),
            pltpu.VMEM((hidden, slots), F32),
            pltpu.VMEM((hidden, slots), F32),
            pltpu.VMEM((hidden, slots), BF16),
            pltpu.VMEM((hidden, slots), BF16),
            pltpu.VMEM((4 * CHANNELS, slots), BF16),
            pltpu.VMEM((8, height), F32),
            pltpu.VMEM((hidden + 16, hidden), F32),
            pltpu.VMEM((enc, hidden), BF16),
            pltpu.VMEM((hidden, hidden), BF16),
            pltpu.VMEM((hidden, tall), BF16),
            pltpu.VMEM((hidden, hidden), BF16),
            pltpu.VMEM((hidden, 4 * CHANNELS), BF16),
            pltpu.VMEM((hidden, lanes), F32),
            pltpu.VMEM((enc, hidden), BF16),
            pltpu.VMEM((hidden, hidden), BF16),
            pltpu.VMEM((16, hidden), F32),
            pltpu.SemaphoreType.DMA((11,)),
            pltpu.SemaphoreType.DMA((9,)),
            pltpu.SemaphoreType.DMA((9,)),
            pltpu.SemaphoreType.DMA((2, levels_z)),
            pltpu.SemaphoreType.DMA((3,)),
        ],
        compiler_params=pltpu.CompilerParams(
            collective_id=0, has_side_effects=True, vmem_limit_bytes=VMEM_BYTES
        ),
        cost_estimate=pl.CostEstimate(flops=flops, bytes_accessed=1 << 21, transcendentals=slots * hidden * 2),
    )(
        ids.reshape(rays, samples),
        positions,
        spacing,
        lengths.reshape(1, rays),
        color_grad,
        w1,
        b1,
        w2,
        b2,
        w3,
        b3,
    )
    shapes = [g1.shape, b1.shape, g2.shape, b2.shape, w3.shape, b3.shape]
    return tuple(
        pl.pallas_call(
            finish,
            out_shape=[jax.ShapeDtypeStruct(shape, F32) for shape in shapes],
            in_specs=[hbm] * 3,
            out_specs=[hbm] * 6,
            scratch_shapes=[pltpu.VMEM(piece.shape, piece.dtype) for piece in (g1, g2, gs)]
            + [pltpu.VMEM(shape, F32) for shape in shapes]
            + [
                pltpu.SemaphoreType.DMA((2 * blocks + 1,)),
                pltpu.SemaphoreType.DMA((2 * blocks + 4,)),
            ],
            compiler_params=pltpu.CompilerParams(vmem_limit_bytes=VMEM_BYTES),
        )(g1, g2, gs)
    )


def solution(mesh):
    copies, cells = mesh.shape["grp"], mesh.shape["cell"]
    levels_z = 16 if cells % 16 == 0 and cells >= 128 else 2
    in_specs = (
        P(("grp", "cell"), None, None),
        P(None, ("grp", "cell"), None),
        P(("grp", "cell"), None),
        P(("grp", "cell")),
        P(None, ("grp", "cell")),
        P("cell", None, None),
        P("cell", None),
        P("cell", None, None),
        P("cell", None),
        P("cell", None, None),
        P("cell", None),
    )
    out_specs = (
        P("cell", None, None),
        P("cell", None),
        P("cell", None, None),
        P("cell", None),
        P("cell", None, None),
        P("cell", None),
    )
    return jax.shard_map(
        functools.partial(local, levels_z, copies),
        mesh=mesh,
        in_specs=in_specs,
        out_specs=out_specs,
        check_vma=False,
    )
```

```python
import functools
import math

import jax
import jax.numpy as jnp
from jax import lax
from jax.experimental import pallas as pl
from jax.experimental.pallas import tpu as pltpu
from jax.sharding import PartitionSpec as P

MESH = pl.DeviceIdType.MESH
F32 = jnp.float32
BF16 = jnp.bfloat16

CHANNELS = 4
RANKS = 8
LEVELS = 16
VMEM_BYTES = 64 * 1024 * 1024 - 64 * 1024
SINE = (6.283164044295505, -41.33714237020527, 81.34076885897593, -70.99343300945087)

NN = (((1,), (0,)), ((), ()))
NT = (((1,), (1,)), ((), ()))


def matmul(a, b, dims=NN):
    return lax.dot_general(a, b, dims, preferred_element_type=F32)


def turns_cosine(turns):
    rest = turns - jnp.round(turns)
    w = 0.25 - jnp.abs(rest)
    square = w * w
    poly = SINE[3]
    for coefficient in SINE[2::-1]:
        poly = poly * square + coefficient
    return w * poly


def split(values, parts):
    pieces = []
    for _ in range(parts - 1):
        piece = values.astype(BF16).astype(F32)
        pieces.append(piece)
        values = values - piece
    pieces.append(values)
    return pieces


def column(row):
    n = row.shape[1]
    diagonal = lax.broadcasted_iota(jnp.int32, (n, n), 0) == lax.broadcasted_iota(
        jnp.int32, (n, n), 1
    )
    return jnp.sum(jnp.where(diagonal, jnp.broadcast_to(row, (n, n)), 0.0), axis=1, keepdims=True)


def swap(tiles):
    lanes = tiles.shape[2]
    part = lanes // 8
    sub = lax.broadcasted_iota(jnp.int32, tiles.shape, 1)
    lane = lax.broadcasted_iota(jnp.int32, tiles.shape, 2) // part
    for bit in (1, 2, 4):
        low = pltpu.roll(pltpu.roll(tiles, 8 - bit, 1), bit * part, 2)
        high = pltpu.roll(pltpu.roll(tiles, bit, 1), lanes - bit * part, 2)
        sub_set = (sub & bit) != 0
        lane_set = (lane & bit) != 0
        moved = jnp.where(lane_set, low, high)
        tiles = jnp.where(sub_set == lane_set, tiles, moved)
    return tiles


def kernel(
    sizes,
    ids_hbm,
    positions_hbm,
    spacing_hbm,
    lengths_hbm,
    color_grad_hbm,
    w1_hbm,
    b1_hbm,
    w2_hbm,
    b2_hbm,
    w3_hbm,
    b3_hbm,
    g1_out,
    g2_out,
    gs_out,
    ids_ref,
    positions_ref,
    spacing_ref,
    lengths_ref,
    color_grad_ref,
    b1_ref,
    b2_ref,
    w3_ref,
    b3_ref,
    v8,
    av,
    bt2,
    asend1,
    arecv1,
    bsend1,
    brecv1,
    bsend2,
    brecv2,
    asend2,
    arecv2,
    asend3,
    arecv3,
    bsend3,
    brecv3,
    feat,
    act1,
    act2,
    slope1,
    slope2,
    delta1,
    delta2,
    og16,
    og_sum,
    second_sum,
    w1_own,
    w2_own,
    w1t,
    w2t,
    w3t,
    b2_wide,
    g1_own,
    g2_own,
    gs_own,
    load_sem,
    send_sem,
    recv_sem,
    near_sem,
    ring_sem,
    all_in_sem,
    own_sem,
):
    copies, group, levels_z, rays, samples = sizes
    inner = group // copies
    lanes = 2 * samples
    rows = rays // 2
    total = rays * samples
    width = levels_z * RANKS
    height = group * CHANNELS
    slots = group * width
    hidden = w2_own.shape[0]
    enc = w1_own.shape[0]

    y = lax.axis_index("grp")
    cell = lax.axis_index("cell")
    z = cell // inner
    inside = cell % inner
    me = y * inner + inside

    def device_a(peer):
        return {"grp": peer // inner, "cell": z * inner + peer % inner}

    def device_b(peer):
        return {"grp": y, "cell": peer * inner + inside}

    loads = [
        pltpu.make_async_copy(source, target, load_sem.at[i])
        for i, (source, target) in enumerate(
            (
                (ids_hbm, ids_ref),
                (positions_hbm, positions_ref),
                (w2_hbm.at[y], w2_own),
                (w1_hbm.at[y], w1_own),
                (b1_hbm, b1_ref),
                (b2_hbm, b2_ref),
                (w3_hbm, w3_ref),
                (b3_hbm, b3_ref),
                (spacing_hbm, spacing_ref),
                (lengths_hbm, lengths_ref),
                (color_grad_hbm, color_grad_ref),
            )
        )
    ]
    loads[0].start()
    loads[1].start()

    barrier = pltpu.get_barrier_semaphore()
    reach = max(1, levels_z // 4)

    def greet_a(k, carry):
        pl.semaphore_signal(
            barrier, inc=1, device_id=device_a((me + k) % group), device_id_type=MESH
        )
        return carry

    def far_first(k):
        left = levels_z - k
        odd = left % 2
        return (z + odd * ((left + 1) // 2) + (1 - odd) * (levels_z - left // 2)) % levels_z

    def greet_b(k, carry):
        for peer in ((z + reach + 1 - k) % levels_z, (z + levels_z - reach - 1 + k) % levels_z):
            pl.semaphore_signal(barrier, inc=1, device_id=device_b(peer), device_id_type=MESH)
        return carry

    lax.fori_loop(1, reach + 1, greet_b, 0)
    lax.fori_loop(1, group, greet_a, 0)
    for load in loads[2:]:
        load.start()
    loads[0].wait()

    def send(source, target, index, own, peer, device, arrived):
        pltpu.make_async_remote_copy(
            src_ref=source.at[peer],
            dst_ref=target.at[own],
            send_sem=send_sem.at[index],
            recv_sem=arrived,
            device_id=device,
            device_id_type=MESH,
        ).start()

    def wait_all(buffer, count, sem):
        others = buffer.at[pl.ds(0, count - 1)]
        pltpu.make_async_copy(others, others, sem).wait()

    def send_a(source, target, index):
        target[me] = source[me]

        def step(k, carry):
            peer = (me + k) % group
            send(source, target, index, me, peer, device_a(peer), recv_sem.at[index])
            return carry

        lax.fori_loop(1, group, step, 0)

    def wait_a(target, index):
        wait_all(target, group, recv_sem.at[index])

    def send_b(source, target, index, row):
        target[z] = source[z]

        def step(k, carry):
            peer = far_first(k)
            send(source, target, index, z, peer, device_b(peer), near_sem.at[row, z])
            return carry

        lax.fori_loop(1, levels_z, step, 0)

    def arrival(target, row, peer):
        pltpu.make_async_copy(target.at[peer], target.at[peer], near_sem.at[row, peer]).wait()

    def pair(values):
        return jnp.concatenate([values[:rows], values[rows:]], axis=1)

    ids = pair(ids_ref[...])
    ids_f = ids.astype(F32)
    square = ids_f
    if rows < lanes:
        square = jnp.concatenate([ids_f, jnp.full((lanes - rows, lanes), -1.0, F32)], axis=0)
    columns = square.T
    earlier = lax.broadcasted_iota(jnp.int32, (lanes, lanes), 0) < lax.broadcasted_iota(
        jnp.int32, (lanes, lanes), 1
    )
    id_rows = [ids_f[g : g + 1] for g in range(rows)]
    counts = [jnp.zeros((8, lanes), F32) for _ in range(rows)]
    for first in range(rows):
        wide = jnp.broadcast_to(columns[:, first : first + 1], (lanes, lanes))
        for g in range(first, rows):
            same = wide == id_rows[g]
            if g == first:
                same = same & earlier
            hits = jnp.where(same, 1.0, 0.0)
            counts[g] = counts[g] + jnp.sum(hits.reshape(lanes // 8, 8, lanes), axis=0)
    owner = ids // copies
    key_a = (ids % copies) * inner + owner % inner
    key_b = (owner // inner) * RANKS
    keys_a = [key_a[g : g + 1] for g in range(rows)]
    slot_row = lax.broadcasted_iota(jnp.int32, (width, lanes), 0)
    owner_row = lax.broadcasted_iota(jnp.int32, (height, lanes), 0) // CHANNELS
    for g in range(rows):
        rank = jnp.sum(counts[g], axis=0, keepdims=True).astype(jnp.int32)
        hit = jnp.where(slot_row == key_b[g : g + 1] + rank, 1.0, 0.0).astype(BF16)
        bt2[0:width, g * lanes : (g + 1) * lanes] = hit
        bt2[width : 2 * width, g * lanes : (g + 1) * lanes] = hit

    def spread(channels, parts):
        for c in range(CHANNELS):
            values = channels[c]
            v8[:, c, :] = values
            v8[:, c + CHANNELS, :] = values
        for g in range(rows):
            mine = owner_row == keys_a[g]
            for p, piece in enumerate(split(v8[g], parts)):
                tall = jnp.concatenate([piece] * (height // 8), axis=0)
                av[p * height : (p + 1) * height, g * lanes : (g + 1) * lanes] = jnp.where(
                    mine, tall, 0.0
                ).astype(BF16)
        wide = matmul(av[0 : parts * height], bt2[0:width], NT)
        result = wide[0:height]
        for p in range(1, parts):
            result = result + wide[p * height : (p + 1) * height]
        return result

    half = group // 2

    def put_a(target, values):
        for j in range(group):
            target[j] = values[j * CHANNELS : (j + 1) * CHANNELS]

    def get_a(source):
        return jnp.concatenate([source[j] for j in range(group)], axis=0)

    def a_to_b(arrived, target):
        tall = jnp.concatenate(
            [
                arrived[h * half : (h + 1) * half, c, :]
                for h in range(2)
                for c in range(CHANNELS)
            ],
            axis=0,
        )
        target[...] = swap(tall.T.reshape(levels_z, RANKS, height))

    def b_to_a(arrived, target):
        tall = swap(arrived[...]).reshape(width, height).T
        for h in range(2):
            for c in range(CHANNELS):
                at = (h * CHANNELS + c) * half
                target[h * half : (h + 1) * half, c, :] = tall[at : at + half]

    loads[1].wait()
    positions = [pair(positions_ref[k]) for k in range(3)]
    put_a(asend1, spread(positions + [jnp.zeros((rows, lanes), F32)], 3))

    pl.semaphore_wait(barrier, group - 1 + 2 * reach)
    for peer in ((z + reach) % levels_z, (z + levels_z - reach) % levels_z):
        pl.semaphore_signal(all_in_sem, inc=1, device_id=device_b(peer), device_id_type=MESH)
    send_a(asend1, arecv1, 0)

    for load in loads[2:]:
        load.wait()
    tall = feat.shape[0]
    b1 = b1_ref[pl.ds(y, 1), :]
    bias_rows = [piece for piece in split(b1, 3)]
    w1_all = jnp.concatenate(
        [w1_own[...].astype(F32)] + bias_rows + [jnp.zeros((tall - enc - 3, hidden), F32)], axis=0
    )
    w1t[...] = (w1_all * 0.5).T.astype(BF16)
    w2t[...] = (w2_own[...].astype(F32) * 0.5).T.astype(BF16)
    w3 = w3_ref[y].astype(F32)
    w3_tall = jnp.concatenate([w3, w3, jnp.zeros((lanes - 2 * CHANNELS, hidden), F32)], axis=0)
    w3t[...] = w3_tall.T[:, 0 : 4 * CHANNELS].astype(BF16)
    w3_rows = jnp.concatenate([w3, jnp.zeros((3 * CHANNELS, hidden), F32)], axis=0).astype(BF16)
    b2_wide[...] = jnp.broadcast_to(b2_ref[pl.ds(y, 1), :] * 0.5, (lanes, hidden)).T
    b3 = column(b3_ref[pl.ds(y, 1), :])
    one_row = lax.broadcasted_iota(jnp.int32, (tall - enc, slots), 0) < 3
    feat[enc:tall, :] = jnp.where(one_row, 1.0, 0.0).astype(BF16)
    act1[hidden:, :] = jnp.ones((act1.shape[0] - hidden, slots), BF16)

    second_sum[...] = jnp.zeros(second_sum.shape, F32)
    og_sum[...] = jnp.zeros(og_sum.shape, F32)

    wait_a(arecv1, 0)
    a_to_b(arecv1, bsend1)
    pl.semaphore_wait(all_in_sem, 2)
    send_b(bsend1, brecv1, 1, 0)

    lane_tile = height
    level = lax.broadcasted_iota(jnp.int32, (3 * LEVELS, lane_tile), 0) % LEVELS
    half_turns = jnp.left_shift(1, level // 2).astype(F32) * jnp.where(
        level % 2 == 1, 0.5 * math.sqrt(2.0), 0.5
    )
    source_lanes = 2 * lane_tile
    pairs = levels_z // 2 - 1
    own_start, far_start = 2 * pairs * source_lanes, (2 * pairs + 1) * source_lanes
    far = (z + levels_z // 2) % levels_z

    def pair_at(d):
        return ((z + d) % levels_z, (z + levels_z - d) % levels_z), 2 * source_lanes * (d - 1)

    def window(start, count):
        if not isinstance(start, int):
            start = pl.multiple_of(start, source_lanes)
        return pl.ds(start, count * source_lanes)

    def encode(tiles):
        tall_point = jnp.concatenate(
            [
                jnp.concatenate(
                    [
                        jnp.broadcast_to(
                            tile[h * CHANNELS + k : h * CHANNELS + k + 1], (LEVELS, lane_tile)
                        )
                        for k in range(3)
                    ],
                    axis=0,
                )
                for tile in tiles
                for h in range(2)
            ],
            axis=1,
        )
        turns = tall_point * jnp.concatenate([half_turns] * (2 * len(tiles)), axis=1)
        return jnp.concatenate([turns_cosine(turns - 0.25), turns_cosine(turns)], axis=0).astype(
            BF16
        )

    def activate(half, act, slope, at):
        slope[:, at] = half
        active = (half + half * jnp.tanh(half)).astype(BF16)
        act[0:hidden, at] = active
        return active

    def forward(peers, start):
        at = window(start, len(peers))
        feat[0:enc, at] = encode([brecv1[peer] for peer in peers])
        first = activate(matmul(w1t[...], feat[:, at]), act1, slope1, at)
        bias = jnp.concatenate([b2_wide[...]] * (len(peers) * source_lanes // lanes), axis=1)
        second = activate(matmul(w2t[...], first) + bias, act2, slope2, at)
        out = matmul(w3_rows, second)[0:CHANNELS] + b3
        for s, peer in enumerate(peers):
            base = s * source_lanes
            bsend2[peer] = jnp.concatenate(
                [
                    out[:, base : base + lane_tile],
                    out[:, base + lane_tile : base + source_lanes],
                ],
                axis=0,
            )

    def forward_remote(peers, start):
        for peer in peers:
            arrival(brecv1, 0, peer)
        forward(peers, start)
        for peer in peers:
            send(bsend2, brecv2, 2, z, peer, device_b(peer), recv_sem.at[2])

    def forward_pair(d, carry):
        forward_remote(*pair_at(d))
        return carry

    forward([z], own_start)
    lax.fori_loop(1, pairs, forward_pair, 0)
    forward_remote([far], far_start)
    if pairs > 0:
        forward_remote(*pair_at(pairs))

    def slope_step(i, carry):
        at = window(i * source_lanes, 1)
        for slope in (slope1, slope2):
            half = slope[:, at]
            bent = jnp.tanh(half)
            slope[:, at] = ((half + 1.0) - half * bent) * (0.5 * bent + 0.5)
        return carry

    lax.fori_loop(0, levels_z, slope_step, 0)

    brecv2[z] = bsend2[z]
    wait_all(brecv2, levels_z, recv_sem.at[2])
    b_to_a(brecv2, asend2)
    send_a(asend2, arecv2, 3)
    wait_a(arecv2, 3)
    returned = jnp.concatenate(split(get_a(arecv2), 2), axis=1).astype(BF16)
    for g in range(rows):
        at = slice(g * lanes, (g + 1) * lanes)
        found = matmul(returned, bt2[:, at])
        kept = jnp.where(owner_row == keys_a[g], found, 0.0)
        both = jnp.sum(kept.reshape(height // 8, 8, lanes), axis=0)
        v8[g] = both
    field = [v8[:, c, :] + v8[:, c + CHANNELS, :] for c in range(CHANNELS)]

    lane = lax.broadcasted_iota(jnp.int32, (rows, lanes), 1)
    left = lane < samples

    def per_ray(row):
        tall_row = column(row)
        return jnp.where(left, tall_row[:rows], tall_row[rows:])

    lengths = per_ray(lengths_ref[...].astype(F32))
    tint = [per_ray(color_grad_ref[c : c + 1, :]) for c in range(3)]
    spacing = pair(spacing_ref[...])
    before = lax.broadcasted_iota(jnp.int32, (lanes, lanes), 0)
    after = lax.broadcasted_iota(jnp.int32, (lanes, lanes), 1)
    same_ray = (before // samples) == (after // samples)

    def scan(values, mask):
        ones = jnp.where(mask & same_ray, 1.0, 0.0).astype(BF16)
        pieces = jnp.concatenate(split(values, 3), axis=0).astype(BF16)
        sums = matmul(pieces, ones)
        return sums[0:rows] + sums[rows : 2 * rows] + sums[2 * rows : 3 * rows]

    live = (lane % samples).astype(F32) < lengths
    density = jnp.maximum(field[0], 0.0) + jnp.log1p(jnp.exp(-jnp.abs(field[0])))
    step = jnp.where(live, density * spacing, 0.0)
    left_over = jnp.exp(-step)
    series = step * (
        1.0 - step * (1 / 2) * (1.0 - step * (1 / 3) * (1.0 - step * (1 / 4) * (1.0 - step * (1 / 5))))
    )
    absorbed = jnp.where(step < 0.05, series, 1.0 - left_over)
    trans = jnp.exp(-scan(step, before < after))
    weight = trans * absorbed
    shade = [0.5 + 0.5 * jnp.tanh(0.5 * field[c]) for c in range(1, CHANNELS)]
    seen = tint[0] * shade[0] + tint[1] * shade[1] + tint[2] * shade[2]
    behind = scan(weight * seen, before > after)
    step_grad = trans * left_over * seen - behind
    density_slope = 0.5 + 0.5 * jnp.tanh(0.5 * field[0])
    out_grad = [jnp.where(live, step_grad * spacing * density_slope, 0.0)]
    for c in range(3):
        out_grad.append(weight * tint[c] * shade[c] * (1.0 - shade[c]))

    put_a(asend3, spread(out_grad, 2))
    send_a(asend3, arecv3, 4)
    wait_a(arecv3, 4)
    a_to_b(arecv3, bsend3)
    send_b(bsend3, brecv3, 5, 1)

    def backward_second(peers, start):
        at = window(start, len(peers))
        tiles = [brecv3[peer] for peer in peers]
        for tile in tiles:
            og_sum[...] = og_sum[...] + tile
        grad = jnp.concatenate(
            [tile[h * CHANNELS : (h + 1) * CHANNELS] for tile in tiles for h in range(2)], axis=1
        )
        pieces = jnp.concatenate(
            split(grad, 2) + [jnp.zeros((2 * CHANNELS, grad.shape[1]), F32)], axis=0
        ).astype(BF16)
        og16[:, at] = pieces
        delta = (matmul(w3t[...], pieces) * slope2[:, at]).astype(BF16)
        delta2[:, at] = delta
        second_sum[...] = second_sum[...] + matmul(act1[:, at], delta, NT)

    def backward_pair(d, carry):
        peers, start = pair_at(d)
        for peer in peers:
            arrival(brecv3, 1, peer)
        backward_second(peers, start)
        return carry

    backward_second([z], own_start)
    lax.fori_loop(1, pairs + 1, backward_pair, 0)
    arrival(brecv3, 1, far)
    backward_second([far], far_start)
    second = second_sum[...]
    g2_own[...] = second[0:hidden].astype(BF16)

    above, below, across = [(y + k) % copies for k in (1, copies - 1, 2)]

    def at_half(ref, part):
        size = ref.shape[0] // 2
        return ref.at[pl.ds(part * size, size)]

    def move(source, target, index, arrived, peer):
        pltpu.make_async_remote_copy(
            src_ref=source,
            dst_ref=target,
            send_sem=send_sem.at[6 + index],
            recv_sem=arrived,
            device_id={"grp": peer, "cell": cell},
            device_id_type=MESH,
        ).start()

    def share(own, out, index):
        pltpu.make_async_copy(own, out.at[y], own_sem.at[index]).start()
        for up, down in ((0, 1), (1, 0)):
            up_half, down_half = at_half(own, up), at_half(own, down)
            move(up_half, at_half(out.at[y], up), index, ring_sem.at[index, up], above)
            move(down_half, at_half(out.at[y], down), index, ring_sem.at[index, 2 + down], below)

    def landed(out, index, slot, part, block):
        half_ref = at_half(out.at[block], part)
        pltpu.make_async_copy(half_ref, half_ref, ring_sem.at[index, slot]).wait()

    def pass_on(out, index):
        landed(out, index, 0, 0, below)
        half_ref = at_half(out.at[below], 0)
        move(half_ref, half_ref, index, ring_sem.at[index, 4], above)
        landed(out, index, 3, 1, above)
        half_ref = at_half(out.at[above], 1)
        move(half_ref, half_ref, index, ring_sem.at[index, 5], below)

    def gathered(own, out, index):
        pltpu.make_async_copy(own, out.at[y], own_sem.at[index]).wait()
        landed(out, index, 1, 1, below)
        landed(out, index, 2, 0, above)
        landed(out, index, 4, 0, across)
        landed(out, index, 5, 1, across)
        wait_all(out, copies, send_sem.at[6 + index])

    share(g2_own, g2_out, 0)

    step_lanes = 2 * source_lanes

    def backward_first(i, carry):
        at = pl.ds(pl.multiple_of(i * step_lanes, step_lanes), step_lanes)
        delta1[:, at] = (matmul(w2_own[...], delta2[:, at]) * slope1[:, at]).astype(BF16)
        return carry

    lax.fori_loop(0, levels_z // 2, backward_first, 0)
    first = matmul(feat[...], delta1[...], NT)
    g1_own[...] = first[0:enc].astype(BF16)
    share(g1_own, g1_out, 1)
    pass_on(g2_out, 0)
    third = matmul(og16[...], act2[...], NT)
    og_total = jnp.sum(og_sum[...], axis=1, keepdims=True)
    og_total = og_total[0:CHANNELS] + og_total[CHANNELS : 2 * CHANNELS]
    diagonal = lax.broadcasted_iota(jnp.int32, (CHANNELS, hidden), 0) == lax.broadcasted_iota(
        jnp.int32, (CHANNELS, hidden), 1
    )
    third_bias = jnp.sum(
        jnp.where(diagonal, jnp.broadcast_to(og_total, (CHANNELS, hidden)), 0.0),
        axis=0,
        keepdims=True,
    )
    gs_own[...] = jnp.concatenate(
        [
            first[enc : enc + 1],
            second[hidden : hidden + 1],
            jnp.zeros((2, hidden), F32),
            third[0:CHANNELS] + third[CHANNELS : 2 * CHANNELS],
            third_bias,
            jnp.zeros((7, hidden), F32),
        ],
        axis=0,
    )
    pltpu.make_async_copy(gs_own, gs_out.at[y], own_sem.at[2]).start()
    for peer in (across, above, below):
        move(gs_own, gs_out.at[y], 2, recv_sem.at[8], peer)
    pass_on(g1_out, 1)

    gathered(g2_own, g2_out, 0)
    gathered(g1_own, g1_out, 1)
    pltpu.make_async_copy(gs_own, gs_out.at[y], own_sem.at[2]).wait()
    wait_all(gs_out, copies, recv_sem.at[8])
    wait_all(gs_out, copies, send_sem.at[8])
    wait_all(asend1, group, send_sem.at[0])
    wait_all(bsend1, levels_z, send_sem.at[1])
    wait_all(bsend2, levels_z, send_sem.at[2])
    wait_all(asend2, group, send_sem.at[3])
    wait_all(asend3, group, send_sem.at[4])
    wait_all(bsend3, levels_z, send_sem.at[5])


def finish(
    g1, g2, gs, g1_out, b1_out, g2_out, b2_out, g3_out, b3_out,
    g1_b, g2_b, gs_b, g1_f, b1_f, g2_f, b2_f, g3_f, b3_f, load_sems, sems
):
    copies = []

    def put(source, target):
        copy = pltpu.make_async_copy(source, target, sems.at[len(copies)])
        copy.start()
        copies.append(copy)

    blocks = g1.shape[0]
    loads = [pltpu.make_async_copy(gs, gs_b, load_sems.at[2 * blocks])]
    for b in range(blocks):
        loads.append(pltpu.make_async_copy(g2.at[b], g2_b.at[b], load_sems.at[2 * b]))
        loads.append(pltpu.make_async_copy(g1.at[b], g1_b.at[b], load_sems.at[2 * b + 1]))
    for load in loads:
        load.start()
    loads[0].wait()
    for b in range(blocks):
        b1_f[b : b + 1, :] = gs_b[b, 0:1, :]
        b2_f[b : b + 1, :] = gs_b[b, 1:2, :]
        g3_f[b] = gs_b[b, 4:8, :]
        b3_f[b : b + 1, :] = gs_b[b, 8:9, 0 : b3_f.shape[1]]
    put(b1_f, b1_out)
    put(b2_f, b2_out)
    put(g3_f, g3_out)
    put(b3_f, b3_out)
    for b in range(blocks):
        loads[1 + 2 * b].wait()
        g2_f[b] = g2_b[b].astype(F32)
        put(g2_f.at[b], g2_out.at[b])
        loads[2 + 2 * b].wait()
        g1_f[b] = g1_b[b].astype(F32)
        put(g1_f.at[b], g1_out.at[b])
    for copy in copies:
        copy.wait()


def local(levels_z, copies, *args):
    (ids, positions, spacing, lengths, color_grad, w1, b1, w2, b2, w3, b3) = args
    rays, samples = spacing.shape
    inner = lax.axis_size("cell") // levels_z
    group = copies * inner
    width = levels_z * RANKS
    height = group * CHANNELS
    slots = group * width
    blocks, enc, hidden = w1.shape
    total = rays * samples
    lanes = 2 * samples
    rows = rays // 2
    tall = enc + 16
    hbm = pl.BlockSpec(memory_space=pltpu.HBM)
    part_a = pltpu.VMEM((group, CHANNELS, width), F32)
    part_b = pltpu.VMEM((levels_z, RANKS, height), F32)
    flops = 2 * slots * (3 * hidden * hidden + 3 * enc * hidden)
    g1, g2, gs = pl.pallas_call(
        functools.partial(kernel, (copies, group, levels_z, rays, samples)),
        out_shape=[
            jax.ShapeDtypeStruct((blocks, enc, hidden), BF16),
            jax.ShapeDtypeStruct((blocks, hidden, hidden), BF16),
            jax.ShapeDtypeStruct((blocks, 16, hidden), F32),
        ],
        in_specs=[hbm] * 11,
        out_specs=[hbm] * 3,
        scratch_shapes=[
            pltpu.VMEM((rays, samples), jnp.int32),
            pltpu.VMEM((3, rays, samples), F32),
            pltpu.VMEM((rays, samples), F32),
            pltpu.VMEM((1, rays), jnp.int32),
            pltpu.VMEM((3, rays), F32),
            pltpu.VMEM(b1.shape, F32),
            pltpu.VMEM(b2.shape, F32),
            pltpu.VMEM(w3.shape, BF16),
            pltpu.VMEM(b3.shape, F32),
            pltpu.VMEM((rows, 8, lanes), F32),
            pltpu.VMEM((3 * height, total), BF16),
            pltpu.VMEM((2 * width, total), BF16),
            part_a,
            part_a,
            part_b,
            part_b,
            part_b,
            part_b,
            part_a,
            part_a,
            part_a,
            part_a,
            part_b,
            part_b,
            pltpu.VMEM((tall, slots), BF16),
            pltpu.VMEM((hidden + 16, slots), BF16),
            pltpu.VMEM((hidden, slots), BF16),
            pltpu.VMEM((hidden, slots), F32),
            pltpu.VMEM((hidden, slots), F32),
            pltpu.VMEM((hidden, slots), BF16),
            pltpu.VMEM((hidden, slots), BF16),
            pltpu.VMEM((4 * CHANNELS, slots), BF16),
            pltpu.VMEM((8, height), F32),
            pltpu.VMEM((hidden + 16, hidden), F32),
            pltpu.VMEM((enc, hidden), BF16),
            pltpu.VMEM((hidden, hidden), BF16),
            pltpu.VMEM((hidden, tall), BF16),
            pltpu.VMEM((hidden, hidden), BF16),
            pltpu.VMEM((hidden, 4 * CHANNELS), BF16),
            pltpu.VMEM((hidden, lanes), F32),
            pltpu.VMEM((enc, hidden), BF16),
            pltpu.VMEM((hidden, hidden), BF16),
            pltpu.VMEM((16, hidden), F32),
            pltpu.SemaphoreType.DMA((11,)),
            pltpu.SemaphoreType.DMA((9,)),
            pltpu.SemaphoreType.DMA((9,)),
            pltpu.SemaphoreType.DMA((2, levels_z)),
            pltpu.SemaphoreType.DMA((2, 6)),
            pltpu.SemaphoreType.REGULAR,
            pltpu.SemaphoreType.DMA((3,)),
        ],
        compiler_params=pltpu.CompilerParams(
            collective_id=0, has_side_effects=True, vmem_limit_bytes=VMEM_BYTES
        ),
        cost_estimate=pl.CostEstimate(flops=flops, bytes_accessed=1 << 21, transcendentals=slots * hidden * 2),
    )(
        ids.reshape(rays, samples),
        positions,
        spacing,
        lengths.reshape(1, rays),
        color_grad,
        w1,
        b1,
        w2,
        b2,
        w3,
        b3,
    )
    shapes = [g1.shape, b1.shape, g2.shape, b2.shape, w3.shape, b3.shape]
    return tuple(
        pl.pallas_call(
            finish,
            out_shape=[jax.ShapeDtypeStruct(shape, F32) for shape in shapes],
            in_specs=[hbm] * 3,
            out_specs=[hbm] * 6,
            scratch_shapes=[pltpu.VMEM(piece.shape, piece.dtype) for piece in (g1, g2, gs)]
            + [pltpu.VMEM(shape, F32) for shape in shapes]
            + [
                pltpu.SemaphoreType.DMA((2 * blocks + 1,)),
                pltpu.SemaphoreType.DMA((2 * blocks + 4,)),
            ],
            compiler_params=pltpu.CompilerParams(vmem_limit_bytes=VMEM_BYTES),
        )(g1, g2, gs)
    )


def solution(mesh):
    copies, cells = mesh.shape["grp"], mesh.shape["cell"]
    levels_z = 16 if cells % 16 == 0 and cells >= 128 else 2
    in_specs = (
        P(("grp", "cell"), None, None),
        P(None, ("grp", "cell"), None),
        P(("grp", "cell"), None),
        P(("grp", "cell")),
        P(None, ("grp", "cell")),
        P("cell", None, None),
        P("cell", None),
        P("cell", None, None),
        P("cell", None),
        P("cell", None, None),
        P("cell", None),
    )
    out_specs = (
        P("cell", None, None),
        P("cell", None),
        P("cell", None, None),
        P("cell", None),
        P("cell", None, None),
        P("cell", None),
    )
    return jax.shard_map(
        functools.partial(local, levels_z, copies),
        mesh=mesh,
        in_specs=in_specs,
        out_specs=out_specs,
        check_vma=False,
    )
```

```python
import functools
import math

import jax
import jax.numpy as jnp
from jax import lax
from jax.experimental import pallas as pl
from jax.experimental.pallas import tpu as pltpu
from jax.sharding import PartitionSpec as P

MESH = pl.DeviceIdType.MESH
F32 = jnp.float32
BF16 = jnp.bfloat16

CHANNELS = 4
RANKS = 8
LEVELS = 16
VMEM_BYTES = 64 * 1024 * 1024 - 64 * 1024
SINE = (6.283164044295505, -41.33714237020527, 81.34076885897593, -70.99343300945087)

NN = (((1,), (0,)), ((), ()))
NT = (((1,), (1,)), ((), ()))


def matmul(a, b, dims=NN):
    return lax.dot_general(a, b, dims, preferred_element_type=F32)


def turns_cosine(turns):
    rest = turns - jnp.round(turns)
    w = 0.25 - jnp.abs(rest)
    square = w * w
    poly = SINE[3]
    for coefficient in SINE[2::-1]:
        poly = poly * square + coefficient
    return w * poly


def split(values, parts):
    pieces = []
    for _ in range(parts - 1):
        piece = values.astype(BF16).astype(F32)
        pieces.append(piece)
        values = values - piece
    pieces.append(values)
    return pieces


def column(row):
    n = row.shape[1]
    diagonal = lax.broadcasted_iota(jnp.int32, (n, n), 0) == lax.broadcasted_iota(
        jnp.int32, (n, n), 1
    )
    return jnp.sum(jnp.where(diagonal, jnp.broadcast_to(row, (n, n)), 0.0), axis=1, keepdims=True)


def swap(tiles):
    lanes = tiles.shape[2]
    part = lanes // 8
    sub = lax.broadcasted_iota(jnp.int32, tiles.shape, 1)
    eighth = lax.broadcasted_iota(jnp.int32, tiles.shape, 2) // part
    apart = (eighth - sub) & 7
    result = tiles
    for d in range(1, 8):
        moved = pltpu.roll(pltpu.roll(tiles, 8 - d, 1), d * part, 2)
        result = jnp.where(apart == d, moved, result)
    return result


def kernel(
    sizes,
    ids_hbm,
    positions_hbm,
    spacing_hbm,
    lengths_hbm,
    color_grad_hbm,
    w1_hbm,
    b1_hbm,
    w2_hbm,
    b2_hbm,
    w3_hbm,
    b3_hbm,
    g1_out,
    g2_out,
    gs_out,
    ids_ref,
    positions_ref,
    spacing_ref,
    lengths_ref,
    color_grad_ref,
    b1_ref,
    b2_ref,
    w3_ref,
    b3_ref,
    v8,
    av,
    bt2,
    asend1,
    arecv1,
    bsend1,
    brecv1,
    bsend2,
    brecv2,
    asend2,
    arecv2,
    asend3,
    arecv3,
    bsend3,
    brecv3,
    feat,
    act1,
    act2,
    slope1,
    slope2,
    delta1,
    delta2,
    og16,
    og_sum,
    second_sum,
    w1_own,
    w2_own,
    w1t,
    w2t,
    w3t,
    b2_wide,
    g1_own,
    g2_own,
    gs_own,
    load_sem,
    send_sem,
    recv_sem,
    near_sem,
    ring_sem,
    all_in_sem,
    own_sem,
):
    copies, group, levels_z, rays, samples = sizes
    inner = group // copies
    lanes = 2 * samples
    rows = rays // 2
    total = rays * samples
    width = levels_z * RANKS
    height = group * CHANNELS
    slots = group * width
    hidden = w2_own.shape[0]
    enc = w1_own.shape[0]

    y = lax.axis_index("grp")
    cell = lax.axis_index("cell")
    z = lax.div(cell, jnp.int32(inner))
    inside = cell - z * inner
    me = y * inner + inside
    cores = 2 if inner % 2 == 0 else 1
    ring_x = inner // cores
    x = lax.div(inside, jnp.int32(cores))
    core = inside - x * cores

    def around(place, count):
        return [place] + [lax.rem(place + d, jnp.int32(count)) for d in range(1, count)]

    def hops(d, count):
        return min(d, count - d)

    on_y, on_x, on_core = around(y, copies), around(x, ring_x), around(core, cores)
    on_z = around(z, levels_z)
    steps_a = sorted(
        ((dy, dx, dc) for dy in range(copies) for dx in range(ring_x) for dc in range(cores)),
        key=lambda d: -hops(d[0], copies) - hops(d[1], ring_x),
    )
    peers_a = [
        (on_y[dy], on_x[dx] * cores + on_core[dc]) for dy, dx, dc in steps_a if dy or dx or dc
    ]
    steps_b = sorted(range(1, levels_z), key=lambda d: -hops(d, levels_z))

    def device_b(peer):
        return {"grp": y, "cell": peer * inner + inside}

    loads = [
        pltpu.make_async_copy(source, target, load_sem.at[i])
        for i, (source, target) in enumerate(
            (
                (ids_hbm, ids_ref),
                (positions_hbm, positions_ref),
                (w2_hbm.at[y], w2_own),
                (w1_hbm.at[y], w1_own),
                (b1_hbm, b1_ref),
                (b2_hbm, b2_ref),
                (w3_hbm, w3_ref),
                (b3_hbm, b3_ref),
                (spacing_hbm, spacing_ref),
                (lengths_hbm, lengths_ref),
                (color_grad_hbm, color_grad_ref),
            )
        )
    ]
    loads[0].start()
    loads[1].start()

    barrier = pltpu.get_barrier_semaphore()
    reach = max(1, levels_z // 4)
    near_b = [d for d in steps_b if hops(d, levels_z) <= reach]
    for d in near_b:
        pl.semaphore_signal(barrier, inc=1, device_id=device_b(on_z[d]), device_id_type=MESH)
    for peer_y, peer_in in peers_a:
        pl.semaphore_signal(
            barrier,
            inc=1,
            device_id={"grp": peer_y, "cell": z * inner + peer_in},
            device_id_type=MESH,
        )
    for load in loads[2:]:
        load.start()
    loads[0].wait()

    def send(source, target, index, own, peer, device, arrived):
        pltpu.make_async_remote_copy(
            src_ref=source.at[peer],
            dst_ref=target.at[own],
            send_sem=send_sem.at[index],
            recv_sem=arrived,
            device_id=device,
            device_id_type=MESH,
        ).start()

    def wait_all(buffer, count, sem):
        others = buffer.at[pl.ds(0, count - 1)]
        pltpu.make_async_copy(others, others, sem).wait()

    def send_a(source, target, index):
        target[me] = source[me]

        for peer_y, peer_in in peers_a:
            device = {"grp": peer_y, "cell": z * inner + peer_in}
            send(source, target, index, me, peer_y * inner + peer_in, device, recv_sem.at[index])

    def wait_a(target, index):
        wait_all(target, group, recv_sem.at[index])

    def send_b(source, target, index, row):
        target[z] = source[z]

        for d in steps_b:
            send(source, target, index, z, on_z[d], device_b(on_z[d]), near_sem.at[row, z])

    def arrival(target, row, peer):
        pltpu.make_async_copy(target.at[peer], target.at[peer], near_sem.at[row, peer]).wait()

    def pair(values):
        return jnp.concatenate([values[:rows], values[rows:]], axis=1)

    ids = pair(ids_ref[...])
    ids_f = ids.astype(F32)
    square = ids_f
    if rows < lanes:
        square = jnp.concatenate([ids_f, jnp.full((lanes - rows, lanes), -1.0, F32)], axis=0)
    columns = square.T
    earlier = lax.broadcasted_iota(jnp.int32, (lanes, lanes), 0) < lax.broadcasted_iota(
        jnp.int32, (lanes, lanes), 1
    )
    id_rows = [ids_f[g : g + 1] for g in range(rows)]
    counts = [jnp.zeros((8, lanes), F32) for _ in range(rows)]
    for first in range(rows):
        wide = jnp.broadcast_to(columns[:, first : first + 1], (lanes, lanes))
        for g in range(first, rows):
            same = wide == id_rows[g]
            if g == first:
                same = same & earlier
            hits = jnp.where(same, 1.0, 0.0)
            counts[g] = counts[g] + jnp.sum(hits.reshape(lanes // 8, 8, lanes), axis=0)
    owner = ids // copies
    key_a = (ids % copies) * inner + owner % inner
    key_b = (owner // inner) * RANKS
    keys_a = [key_a[g : g + 1] for g in range(rows)]
    slot_row = lax.broadcasted_iota(jnp.int32, (width, lanes), 0)
    owner_row = lax.broadcasted_iota(jnp.int32, (height, lanes), 0) // CHANNELS
    for g in range(rows):
        rank = jnp.sum(counts[g], axis=0, keepdims=True).astype(jnp.int32)
        hit = jnp.where(slot_row == key_b[g : g + 1] + rank, 1.0, 0.0).astype(BF16)
        bt2[0:width, g * lanes : (g + 1) * lanes] = hit
        bt2[width : 2 * width, g * lanes : (g + 1) * lanes] = hit

    def spread(channels, parts):
        for c in range(CHANNELS):
            values = channels[c]
            v8[:, c, :] = values
            v8[:, c + CHANNELS, :] = values
        for g in range(rows):
            mine = owner_row == keys_a[g]
            for p, piece in enumerate(split(v8[g], parts)):
                tall = jnp.concatenate([piece] * (height // 8), axis=0)
                av[p * height : (p + 1) * height, g * lanes : (g + 1) * lanes] = jnp.where(
                    mine, tall, 0.0
                ).astype(BF16)
        wide = matmul(av[0 : parts * height], bt2[0:width], NT)
        result = wide[0:height]
        for p in range(1, parts):
            result = result + wide[p * height : (p + 1) * height]
        return result

    half = group // 2

    def put_a(target, values):
        for j in range(group):
            target[j] = values[j * CHANNELS : (j + 1) * CHANNELS]

    def get_a(source):
        return jnp.concatenate([source[j] for j in range(group)], axis=0)

    def a_to_b(arrived, target):
        tall = jnp.concatenate(
            [
                arrived[h * half : (h + 1) * half, c, :]
                for h in range(2)
                for c in range(CHANNELS)
            ],
            axis=0,
        )
        target[...] = swap(tall.T.reshape(levels_z, RANKS, height))

    def b_to_a(arrived, target):
        tall = swap(arrived[...]).reshape(width, height).T
        for h in range(2):
            for c in range(CHANNELS):
                at = (h * CHANNELS + c) * half
                target[h * half : (h + 1) * half, c, :] = tall[at : at + half]

    loads[1].wait()
    positions = [pair(positions_ref[k]) for k in range(3)]
    put_a(asend1, spread(positions + [jnp.zeros((rows, lanes), F32)], 3))

    pl.semaphore_wait(barrier, group - 1 + len(near_b))
    for d in (reach, levels_z - reach):
        pl.semaphore_signal(all_in_sem, inc=1, device_id=device_b(on_z[d]), device_id_type=MESH)
    send_a(asend1, arecv1, 0)

    for load in loads[2:]:
        load.wait()
    tall = feat.shape[0]
    b1 = b1_ref[pl.ds(y, 1), :]
    bias_rows = [piece for piece in split(b1, 3)]
    w1_all = jnp.concatenate(
        [w1_own[...].astype(F32)] + bias_rows + [jnp.zeros((tall - enc - 3, hidden), F32)], axis=0
    )
    w1t[...] = (w1_all * 0.5).T.astype(BF16)
    w2t[...] = (w2_own[...].astype(F32) * 0.5).T.astype(BF16)
    w3 = w3_ref[y].astype(F32)
    w3_tall = jnp.concatenate([w3, w3, jnp.zeros((lanes - 2 * CHANNELS, hidden), F32)], axis=0)
    w3t[...] = w3_tall.T[:, 0 : 4 * CHANNELS].astype(BF16)
    w3_rows = jnp.concatenate([w3, jnp.zeros((3 * CHANNELS, hidden), F32)], axis=0).astype(BF16)
    b2_wide[...] = jnp.broadcast_to(b2_ref[pl.ds(y, 1), :] * 0.5, (lanes, hidden)).T
    b3 = column(b3_ref[pl.ds(y, 1), :])
    one_row = lax.broadcasted_iota(jnp.int32, (tall - enc, slots), 0) < 3
    feat[enc:tall, :] = jnp.where(one_row, 1.0, 0.0).astype(BF16)
    act1[hidden:, :] = jnp.ones((act1.shape[0] - hidden, slots), BF16)

    og_sum[...] = jnp.zeros(og_sum.shape, F32)

    wait_a(arecv1, 0)
    a_to_b(arecv1, bsend1)
    pl.semaphore_wait(all_in_sem, 2)
    send_b(bsend1, brecv1, 1, 0)

    lane_tile = height
    level = lax.broadcasted_iota(jnp.int32, (3 * LEVELS, lane_tile), 0) % LEVELS
    half_turns = jnp.left_shift(1, level // 2).astype(F32) * jnp.where(
        level % 2 == 1, 0.5 * math.sqrt(2.0), 0.5
    )
    source_lanes = 2 * lane_tile
    pairs = levels_z // 2 - 1
    own_start, far_start = 2 * pairs * source_lanes, (2 * pairs + 1) * source_lanes
    far = on_z[levels_z // 2]

    def pair_at(d):
        ring = jnp.int32(levels_z)
        return (lax.rem(z + d, ring), lax.rem(z + levels_z - d, ring)), 2 * source_lanes * (d - 1)

    def window(start, count):
        if not isinstance(start, int):
            start = pl.multiple_of(start, source_lanes)
        return pl.ds(start, count * source_lanes)

    def encode(tiles):
        tall_point = jnp.concatenate(
            [
                jnp.concatenate(
                    [
                        jnp.broadcast_to(
                            tile[h * CHANNELS + k : h * CHANNELS + k + 1], (LEVELS, lane_tile)
                        )
                        for k in range(3)
                    ],
                    axis=0,
                )
                for tile in tiles
                for h in range(2)
            ],
            axis=1,
        )
        turns = tall_point * jnp.concatenate([half_turns] * (2 * len(tiles)), axis=1)
        return jnp.concatenate([turns_cosine(turns - 0.25), turns_cosine(turns)], axis=0).astype(
            BF16
        )

    def activate(half, act, slope, at):
        slope[:, at] = half
        active = (half + half * jnp.tanh(half)).astype(BF16)
        act[0:hidden, at] = active
        return active

    def forward(peers, start):
        at = window(start, len(peers))
        feat[0:enc, at] = encode([brecv1[peer] for peer in peers])
        first = activate(matmul(w1t[...], feat[:, at]), act1, slope1, at)
        bias = jnp.concatenate([b2_wide[...]] * (len(peers) * source_lanes // lanes), axis=1)
        second = activate(matmul(w2t[...], first) + bias, act2, slope2, at)
        out = matmul(w3_rows, second)[0:CHANNELS] + b3
        for s, peer in enumerate(peers):
            base = s * source_lanes
            bsend2[peer] = jnp.concatenate(
                [
                    out[:, base : base + lane_tile],
                    out[:, base + lane_tile : base + source_lanes],
                ],
                axis=0,
            )

    def forward_remote(peers, start):
        for peer in peers:
            arrival(brecv1, 0, peer)
        forward(peers, start)
        for peer in peers:
            send(bsend2, brecv2, 2, z, peer, device_b(peer), recv_sem.at[2])

    def forward_pair(d, carry):
        forward_remote(*pair_at(d))
        return carry

    forward([z], own_start)
    lax.fori_loop(1, pairs, forward_pair, 0)
    forward_remote([far], far_start)
    if pairs > 0:
        forward_remote(*pair_at(pairs))

    def slope_step(i, carry):
        at = window(i * source_lanes, 1)
        for slope in (slope1, slope2):
            half = slope[:, at]
            bent = jnp.tanh(half)
            slope[:, at] = ((half + 1.0) - half * bent) * (0.5 * bent + 0.5)
        return carry

    lax.fori_loop(0, levels_z, slope_step, 0)

    lane = lax.broadcasted_iota(jnp.int32, (rows, lanes), 1)
    left = lane < samples

    def per_ray(row):
        tall_row = column(row)
        return jnp.where(left, tall_row[:rows], tall_row[rows:])

    lengths = per_ray(lengths_ref[...].astype(F32))
    tint = [per_ray(color_grad_ref[c : c + 1, :]) for c in range(3)]
    spacing = pair(spacing_ref[...])
    before = lax.broadcasted_iota(jnp.int32, (lanes, lanes), 0)
    after = lax.broadcasted_iota(jnp.int32, (lanes, lanes), 1)
    same_ray = (before // samples) == (after // samples)

    earlier_mask = jnp.where((before < after) & same_ray, 1.0, 0.0).astype(BF16)
    later_mask = jnp.where((before > after) & same_ray, 1.0, 0.0).astype(BF16)

    def scan(values, mask):
        pieces = jnp.concatenate(split(values, 3), axis=0).astype(BF16)
        sums = matmul(pieces, mask)
        return sums[0:rows] + sums[rows : 2 * rows] + sums[2 * rows : 3 * rows]

    live = (lane % samples).astype(F32) < lengths
    brecv2[z] = bsend2[z]
    wait_all(brecv2, levels_z, recv_sem.at[2])
    b_to_a(brecv2, asend2)
    send_a(asend2, arecv2, 3)
    wait_a(arecv2, 3)
    returned = jnp.concatenate(split(get_a(arecv2), 2), axis=1).astype(BF16)
    for g in range(rows):
        at = slice(g * lanes, (g + 1) * lanes)
        found = matmul(returned, bt2[:, at])
        kept = jnp.where(owner_row == keys_a[g], found, 0.0)
        both = jnp.sum(kept.reshape(height // 8, 8, lanes), axis=0)
        v8[g] = both
    field = [v8[:, c, :] + v8[:, c + CHANNELS, :] for c in range(CHANNELS)]

    density = jnp.maximum(field[0], 0.0) + jnp.log1p(jnp.exp(-jnp.abs(field[0])))
    step = jnp.where(live, density * spacing, 0.0)
    left_over = jnp.exp(-step)
    series = step * (
        1.0 - step * (1 / 2) * (1.0 - step * (1 / 3) * (1.0 - step * (1 / 4) * (1.0 - step * (1 / 5))))
    )
    absorbed = jnp.where(step < 0.05, series, 1.0 - left_over)
    trans = jnp.exp(-scan(step, earlier_mask))
    weight = trans * absorbed
    shade = [0.5 + 0.5 * jnp.tanh(0.5 * field[c]) for c in range(1, CHANNELS)]
    seen = tint[0] * shade[0] + tint[1] * shade[1] + tint[2] * shade[2]
    behind = scan(weight * seen, later_mask)
    step_grad = trans * left_over * seen - behind
    density_slope = 0.5 + 0.5 * jnp.tanh(0.5 * field[0])
    out_grad = [jnp.where(live, step_grad * spacing * density_slope, 0.0)]
    for c in range(3):
        out_grad.append(weight * tint[c] * shade[c] * (1.0 - shade[c]))

    put_a(asend3, spread(out_grad, 2))
    send_a(asend3, arecv3, 4)
    wait_a(arecv3, 4)
    a_to_b(arecv3, bsend3)
    send_b(bsend3, brecv3, 5, 1)

    def backward_second(peers, start):
        at = window(start, len(peers))
        tiles = [brecv3[peer] for peer in peers]
        for tile in tiles:
            og_sum[...] = og_sum[...] + tile
        grad = jnp.concatenate(
            [tile[h * CHANNELS : (h + 1) * CHANNELS] for tile in tiles for h in range(2)], axis=1
        )
        pieces = jnp.concatenate(
            split(grad, 2) + [jnp.zeros((2 * CHANNELS, grad.shape[1]), F32)], axis=0
        ).astype(BF16)
        og16[:, at] = pieces
        delta = (matmul(w3t[...], pieces) * slope2[:, at]).astype(BF16)
        delta2[:, at] = delta
        return matmul(act1[:, at], delta, NT)

    def backward_pair(d, carry):
        peers, start = pair_at(d)
        for peer in peers:
            arrival(brecv3, 1, peer)
        second_sum[...] = second_sum[...] + backward_second(peers, start)
        return carry

    second_sum[...] = backward_second([z], own_start)
    lax.fori_loop(1, pairs + 1, backward_pair, 0)
    arrival(brecv3, 1, far)
    second = second_sum[...] + backward_second([far], far_start)
    g2_own[...] = second[0:hidden].astype(BF16)

    above, below, across = on_y[1], on_y[copies - 1], on_y[2]

    def at_half(ref, part):
        size = ref.shape[0] // 2
        return ref.at[pl.ds(part * size, size)]

    def move(source, target, index, arrived, peer):
        pltpu.make_async_remote_copy(
            src_ref=source,
            dst_ref=target,
            send_sem=send_sem.at[6 + index],
            recv_sem=arrived,
            device_id={"grp": peer, "cell": cell},
            device_id_type=MESH,
        ).start()

    def share(own, out, index):
        pltpu.make_async_copy(own, out.at[y], own_sem.at[index]).start()
        for up, down in ((0, 1), (1, 0)):
            up_half, down_half = at_half(own, up), at_half(own, down)
            move(up_half, at_half(out.at[y], up), index, ring_sem.at[index, up], above)
            move(down_half, at_half(out.at[y], down), index, ring_sem.at[index, 2 + down], below)

    def landed(out, index, slot, part, block):
        half_ref = at_half(out.at[block], part)
        pltpu.make_async_copy(half_ref, half_ref, ring_sem.at[index, slot]).wait()

    def pass_on(out, index):
        landed(out, index, 0, 0, below)
        half_ref = at_half(out.at[below], 0)
        move(half_ref, half_ref, index, ring_sem.at[index, 4], above)
        landed(out, index, 3, 1, above)
        half_ref = at_half(out.at[above], 1)
        move(half_ref, half_ref, index, ring_sem.at[index, 5], below)

    def gathered(own, out, index):
        pltpu.make_async_copy(own, out.at[y], own_sem.at[index]).wait()
        landed(out, index, 1, 1, below)
        landed(out, index, 2, 0, above)
        landed(out, index, 4, 0, across)
        landed(out, index, 5, 1, across)
        wait_all(out, copies, send_sem.at[6 + index])

    share(g2_own, g2_out, 0)

    step_lanes = 2 * source_lanes

    def backward_first(i, carry):
        at = pl.ds(pl.multiple_of(i * step_lanes, step_lanes), step_lanes)
        delta1[:, at] = (matmul(w2_own[...], delta2[:, at]) * slope1[:, at]).astype(BF16)
        return carry

    lax.fori_loop(0, levels_z // 2, backward_first, 0)
    first = matmul(feat[...], delta1[...], NT)
    g1_own[...] = first[0:enc].astype(BF16)
    share(g1_own, g1_out, 1)
    pass_on(g2_out, 0)
    third = matmul(og16[...], act2[...], NT)
    og_total = jnp.sum(og_sum[...], axis=1, keepdims=True)
    og_total = og_total[0:CHANNELS] + og_total[CHANNELS : 2 * CHANNELS]
    diagonal = lax.broadcasted_iota(jnp.int32, (CHANNELS, hidden), 0) == lax.broadcasted_iota(
        jnp.int32, (CHANNELS, hidden), 1
    )
    third_bias = jnp.sum(
        jnp.where(diagonal, jnp.broadcast_to(og_total, (CHANNELS, hidden)), 0.0),
        axis=0,
        keepdims=True,
    )
    gs_own[...] = jnp.concatenate(
        [
            first[enc : enc + 1],
            second[hidden : hidden + 1],
            jnp.zeros((2, hidden), F32),
            third[0:CHANNELS] + third[CHANNELS : 2 * CHANNELS],
            third_bias,
            jnp.zeros((7, hidden), F32),
        ],
        axis=0,
    )
    pltpu.make_async_copy(gs_own, gs_out.at[y], own_sem.at[2]).start()
    for peer in (across, above, below):
        move(gs_own, gs_out.at[y], 2, recv_sem.at[8], peer)
    pass_on(g1_out, 1)

    gathered(g2_own, g2_out, 0)
    gathered(g1_own, g1_out, 1)
    pltpu.make_async_copy(gs_own, gs_out.at[y], own_sem.at[2]).wait()
    wait_all(gs_out, copies, recv_sem.at[8])
    wait_all(gs_out, copies, send_sem.at[8])
    wait_all(asend1, group, send_sem.at[0])
    wait_all(bsend1, levels_z, send_sem.at[1])
    wait_all(bsend2, levels_z, send_sem.at[2])
    wait_all(asend2, group, send_sem.at[3])
    wait_all(asend3, group, send_sem.at[4])
    wait_all(bsend3, levels_z, send_sem.at[5])


def finish(
    g1, g2, gs, g1_out, b1_out, g2_out, b2_out, g3_out, b3_out,
    g1_b, g2_b, gs_b, g1_f, b1_f, g2_f, b2_f, g3_f, b3_f, load_sems, sems
):
    copies = []

    def put(source, target):
        copy = pltpu.make_async_copy(source, target, sems.at[len(copies)])
        copy.start()
        copies.append(copy)

    blocks = g1.shape[0]
    loads = [pltpu.make_async_copy(gs, gs_b, load_sems.at[2 * blocks])]
    for b in range(blocks):
        loads.append(pltpu.make_async_copy(g2.at[b], g2_b.at[b], load_sems.at[2 * b]))
        loads.append(pltpu.make_async_copy(g1.at[b], g1_b.at[b], load_sems.at[2 * b + 1]))
    for load in loads:
        load.start()
    loads[0].wait()
    for b in range(blocks):
        b1_f[b : b + 1, :] = gs_b[b, 0:1, :]
        b2_f[b : b + 1, :] = gs_b[b, 1:2, :]
        g3_f[b] = gs_b[b, 4:8, :]
        b3_f[b : b + 1, :] = gs_b[b, 8:9, 0 : b3_f.shape[1]]
    put(b1_f, b1_out)
    put(b2_f, b2_out)
    put(g3_f, g3_out)
    put(b3_f, b3_out)
    for b in range(blocks):
        loads[1 + 2 * b].wait()
        g2_f[b] = g2_b[b].astype(F32)
        put(g2_f.at[b], g2_out.at[b])
        loads[2 + 2 * b].wait()
        g1_f[b] = g1_b[b].astype(F32)
        put(g1_f.at[b], g1_out.at[b])
    for copy in copies:
        copy.wait()


def local(levels_z, copies, *args):
    (ids, positions, spacing, lengths, color_grad, w1, b1, w2, b2, w3, b3) = args
    rays, samples = spacing.shape
    inner = lax.axis_size("cell") // levels_z
    group = copies * inner
    width = levels_z * RANKS
    height = group * CHANNELS
    slots = group * width
    blocks, enc, hidden = w1.shape
    total = rays * samples
    lanes = 2 * samples
    rows = rays // 2
    tall = enc + 16
    hbm = pl.BlockSpec(memory_space=pltpu.HBM)
    part_a = pltpu.VMEM((group, CHANNELS, width), F32)
    part_b = pltpu.VMEM((levels_z, RANKS, height), F32)
    flops = 2 * slots * (3 * hidden * hidden + 3 * enc * hidden)
    g1, g2, gs = pl.pallas_call(
        functools.partial(kernel, (copies, group, levels_z, rays, samples)),
        out_shape=[
            jax.ShapeDtypeStruct((blocks, enc, hidden), BF16),
            jax.ShapeDtypeStruct((blocks, hidden, hidden), BF16),
            jax.ShapeDtypeStruct((blocks, 16, hidden), F32),
        ],
        in_specs=[hbm] * 11,
        out_specs=[hbm] * 3,
        scratch_shapes=[
            pltpu.VMEM((rays, samples), jnp.int32),
            pltpu.VMEM((3, rays, samples), F32),
            pltpu.VMEM((rays, samples), F32),
            pltpu.VMEM((1, rays), jnp.int32),
            pltpu.VMEM((3, rays), F32),
            pltpu.VMEM(b1.shape, F32),
            pltpu.VMEM(b2.shape, F32),
            pltpu.VMEM(w3.shape, BF16),
            pltpu.VMEM(b3.shape, F32),
            pltpu.VMEM((rows, 8, lanes), F32),
            pltpu.VMEM((3 * height, total), BF16),
            pltpu.VMEM((2 * width, total), BF16),
            part_a,
            part_a,
            part_b,
            part_b,
            part_b,
            part_b,
            part_a,
            part_a,
            part_a,
            part_a,
            part_b,
            part_b,
            pltpu.VMEM((tall, slots), BF16),
            pltpu.VMEM((hidden + 16, slots), BF16),
            pltpu.VMEM((hidden, slots), BF16),
            pltpu.VMEM((hidden, slots), F32),
            pltpu.VMEM((hidden, slots), F32),
            pltpu.VMEM((hidden, slots), BF16),
            pltpu.VMEM((hidden, slots), BF16),
            pltpu.VMEM((4 * CHANNELS, slots), BF16),
            pltpu.VMEM((8, height), F32),
            pltpu.VMEM((hidden + 16, hidden), F32),
            pltpu.VMEM((enc, hidden), BF16),
            pltpu.VMEM((hidden, hidden), BF16),
            pltpu.VMEM((hidden, tall), BF16),
            pltpu.VMEM((hidden, hidden), BF16),
            pltpu.VMEM((hidden, 4 * CHANNELS), BF16),
            pltpu.VMEM((hidden, lanes), F32),
            pltpu.VMEM((enc, hidden), BF16),
            pltpu.VMEM((hidden, hidden), BF16),
            pltpu.VMEM((16, hidden), F32),
            pltpu.SemaphoreType.DMA((11,)),
            pltpu.SemaphoreType.DMA((9,)),
            pltpu.SemaphoreType.DMA((9,)),
            pltpu.SemaphoreType.DMA((2, levels_z)),
            pltpu.SemaphoreType.DMA((2, 6)),
            pltpu.SemaphoreType.REGULAR,
            pltpu.SemaphoreType.DMA((3,)),
        ],
        compiler_params=pltpu.CompilerParams(
            collective_id=0, has_side_effects=True, vmem_limit_bytes=VMEM_BYTES
        ),
        cost_estimate=pl.CostEstimate(flops=flops, bytes_accessed=1 << 21, transcendentals=slots * hidden * 2),
    )(
        ids.reshape(rays, samples),
        positions,
        spacing,
        lengths.reshape(1, rays),
        color_grad,
        w1,
        b1,
        w2,
        b2,
        w3,
        b3,
    )
    shapes = [g1.shape, b1.shape, g2.shape, b2.shape, w3.shape, b3.shape]
    return tuple(
        pl.pallas_call(
            finish,
            out_shape=[jax.ShapeDtypeStruct(shape, F32) for shape in shapes],
            in_specs=[hbm] * 3,
            out_specs=[hbm] * 6,
            scratch_shapes=[pltpu.VMEM(piece.shape, piece.dtype) for piece in (g1, g2, gs)]
            + [pltpu.VMEM(shape, F32) for shape in shapes]
            + [
                pltpu.SemaphoreType.DMA((2 * blocks + 1,)),
                pltpu.SemaphoreType.DMA((2 * blocks + 4,)),
            ],
            compiler_params=pltpu.CompilerParams(vmem_limit_bytes=VMEM_BYTES),
        )(g1, g2, gs)
    )


def solution(mesh):
    copies, cells = mesh.shape["grp"], mesh.shape["cell"]
    levels_z = 16 if cells % 16 == 0 and cells >= 128 else 2
    in_specs = (
        P(("grp", "cell"), None, None),
        P(None, ("grp", "cell"), None),
        P(("grp", "cell"), None),
        P(("grp", "cell")),
        P(None, ("grp", "cell")),
        P("cell", None, None),
        P("cell", None),
        P("cell", None, None),
        P("cell", None),
        P("cell", None, None),
        P("cell", None),
    )
    out_specs = (
        P("cell", None, None),
        P("cell", None),
        P("cell", None, None),
        P("cell", None),
        P("cell", None, None),
        P("cell", None),
    )
    return jax.shard_map(
        functools.partial(local, levels_z, copies),
        mesh=mesh,
        in_specs=in_specs,
        out_specs=out_specs,
        check_vma=False,
    )
```

```python
import functools
import math

import jax
import jax.numpy as jnp
from jax import lax
from jax.experimental import pallas as pl
from jax.experimental.pallas import tpu as pltpu
from jax.sharding import PartitionSpec as P

MESH = pl.DeviceIdType.MESH
F32 = jnp.float32
BF16 = jnp.bfloat16

CHANNELS = 4
RANKS = 8
LEVELS = 16
VMEM_BYTES = 64 * 1024 * 1024 - 64 * 1024
SINE = (6.283164044295505, -41.33714237020527, 81.34076885897593, -70.99343300945087)

NN = (((1,), (0,)), ((), ()))
NT = (((1,), (1,)), ((), ()))


def matmul(a, b, dims=NN):
    return lax.dot_general(a, b, dims, preferred_element_type=F32)


def turns_cosine(turns):
    rest = turns - jnp.round(turns)
    w = 0.25 - jnp.abs(rest)
    square = w * w
    poly = SINE[3]
    for coefficient in SINE[2::-1]:
        poly = poly * square + coefficient
    return w * poly


def split(values, parts):
    pieces = []
    for _ in range(parts - 1):
        piece = values.astype(BF16).astype(F32)
        pieces.append(piece)
        values = values - piece
    pieces.append(values)
    return pieces


def column(row):
    n = row.shape[1]
    diagonal = lax.broadcasted_iota(jnp.int32, (n, n), 0) == lax.broadcasted_iota(
        jnp.int32, (n, n), 1
    )
    return jnp.sum(jnp.where(diagonal, jnp.broadcast_to(row, (n, n)), 0.0), axis=1, keepdims=True)


def swap(tiles):
    lanes = tiles.shape[2]
    part = lanes // 8
    sub = lax.broadcasted_iota(jnp.int32, tiles.shape, 1)
    eighth = lax.broadcasted_iota(jnp.int32, tiles.shape, 2) // part
    apart = (eighth - sub) & 7
    result = tiles
    for d in range(1, 8):
        moved = pltpu.roll(pltpu.roll(tiles, 8 - d, 1), d * part, 2)
        result = jnp.where(apart == d, moved, result)
    return result


def kernel(
    sizes,
    ids_hbm,
    positions_hbm,
    spacing_hbm,
    lengths_hbm,
    color_grad_hbm,
    w1_hbm,
    b1_hbm,
    w2_hbm,
    b2_hbm,
    w3_hbm,
    b3_hbm,
    g1_out,
    g2_out,
    gs_out,
    ids_ref,
    positions_ref,
    spacing_ref,
    lengths_ref,
    color_grad_ref,
    b1_ref,
    b2_ref,
    w3_ref,
    b3_ref,
    v8,
    av,
    bt2,
    bt_turned,
    asend1,
    arecv1,
    bsend1,
    brecv1,
    bsend2,
    brecv2,
    asend2,
    arecv2,
    asend3,
    arecv3,
    bsend3,
    brecv3,
    feat,
    act1,
    act2,
    slope1,
    slope2,
    delta1,
    delta2,
    og16,
    og_sum,
    second_sum,
    w1_own,
    w2_own,
    w1t,
    w2t,
    w3t,
    b2_wide,
    g1_own,
    g2_own,
    gs_own,
    load_sem,
    send_sem,
    recv_sem,
    near_sem,
    ring_sem,
    all_in_sem,
    own_sem,
):
    copies, group, levels_z, rays, samples = sizes
    inner = group // copies
    lanes = 2 * samples
    rows = rays // 2
    total = rays * samples
    width = levels_z * RANKS
    height = group * CHANNELS
    slots = group * width
    hidden = w2_own.shape[0]
    enc = w1_own.shape[0]

    y = lax.axis_index("grp")
    cell = lax.axis_index("cell")
    z = lax.div(cell, jnp.int32(inner))
    inside = cell - z * inner
    me = y * inner + inside
    cores = 2 if inner % 2 == 0 else 1
    ring_x = inner // cores
    x = lax.div(inside, jnp.int32(cores))
    core = inside - x * cores

    def around(place, count):
        return [place] + [lax.rem(place + d, jnp.int32(count)) for d in range(1, count)]

    def hops(d, count):
        return min(d, count - d)

    on_y, on_x, on_core = around(y, copies), around(x, ring_x), around(core, cores)
    on_z = around(z, levels_z)
    steps_a = sorted(
        ((dy, dx, dc) for dy in range(copies) for dx in range(ring_x) for dc in range(cores)),
        key=lambda d: -hops(d[0], copies) - hops(d[1], ring_x),
    )
    peers_a = [
        (on_y[dy], on_x[dx] * cores + on_core[dc]) for dy, dx, dc in steps_a if dy or dx or dc
    ]
    steps_b = sorted(range(1, levels_z), key=lambda d: -hops(d, levels_z))

    def device_b(peer):
        return {"grp": y, "cell": peer * inner + inside}

    loads = [
        pltpu.make_async_copy(source, target, load_sem.at[i])
        for i, (source, target) in enumerate(
            (
                (ids_hbm, ids_ref),
                (positions_hbm, positions_ref),
                (w2_hbm.at[y], w2_own),
                (w1_hbm.at[y], w1_own),
                (b1_hbm, b1_ref),
                (b2_hbm, b2_ref),
                (w3_hbm, w3_ref),
                (b3_hbm, b3_ref),
                (spacing_hbm, spacing_ref),
                (lengths_hbm, lengths_ref),
                (color_grad_hbm, color_grad_ref),
            )
        )
    ]
    loads[0].start()
    loads[1].start()

    barrier = pltpu.get_barrier_semaphore()
    reach = max(1, levels_z // 4)
    near_b = [d for d in steps_b if hops(d, levels_z) <= reach]
    for d in near_b:
        pl.semaphore_signal(barrier, inc=1, device_id=device_b(on_z[d]), device_id_type=MESH)
    for peer_y, peer_in in peers_a:
        pl.semaphore_signal(
            barrier,
            inc=1,
            device_id={"grp": peer_y, "cell": z * inner + peer_in},
            device_id_type=MESH,
        )
    for load in loads[2:]:
        load.start()
    loads[0].wait()

    def send(source, target, index, own, peer, device, arrived):
        pltpu.make_async_remote_copy(
            src_ref=source.at[peer],
            dst_ref=target.at[own],
            send_sem=send_sem.at[index],
            recv_sem=arrived,
            device_id=device,
            device_id_type=MESH,
        ).start()

    def wait_all(buffer, count, sem):
        others = buffer.at[pl.ds(0, count - 1)]
        pltpu.make_async_copy(others, others, sem).wait()

    def send_a(source, target, index):
        for peer_y, peer_in in peers_a:
            device = {"grp": peer_y, "cell": z * inner + peer_in}
            send(source, target, index, me, peer_y * inner + peer_in, device, recv_sem.at[index])
        target[me] = source[me]

    def wait_a(target, index):
        wait_all(target, group, recv_sem.at[index])

    def send_b(source, target, index, row):
        for d in steps_b:
            send(source, target, index, z, on_z[d], device_b(on_z[d]), near_sem.at[row, z])
        target[z] = source[z]

    def arrival(target, row, peer):
        pltpu.make_async_copy(target.at[peer], target.at[peer], near_sem.at[row, peer]).wait()

    def pair(values):
        return jnp.concatenate([values[:rows], values[rows:]], axis=1)

    ids = pair(ids_ref[...])
    ids_f = ids.astype(F32)
    square = ids_f
    if rows < lanes:
        square = jnp.concatenate([ids_f, jnp.full((lanes - rows, lanes), -1.0, F32)], axis=0)
    columns = square.T
    earlier = lax.broadcasted_iota(jnp.int32, (lanes, lanes), 0) < lax.broadcasted_iota(
        jnp.int32, (lanes, lanes), 1
    )
    id_rows = [ids_f[g : g + 1] for g in range(rows)]
    counts = [jnp.zeros((8, lanes), F32) for _ in range(rows)]
    for first in range(rows):
        wide = jnp.broadcast_to(columns[:, first : first + 1], (lanes, lanes))
        for g in range(first, rows):
            same = wide == id_rows[g]
            if g == first:
                same = same & earlier
            hits = jnp.where(same, 1.0, 0.0)
            counts[g] = counts[g] + jnp.sum(hits.reshape(lanes // 8, 8, lanes), axis=0)
    owner = ids // copies
    key_a = (ids % copies) * inner + owner % inner
    key_b = (owner // inner) * RANKS
    keys_a = [key_a[g : g + 1] for g in range(rows)]
    slot_row = lax.broadcasted_iota(jnp.int32, (width, lanes), 0)
    owner_row = lax.broadcasted_iota(jnp.int32, (height, lanes), 0) // CHANNELS
    for g in range(rows):
        rank = jnp.sum(counts[g], axis=0, keepdims=True).astype(jnp.int32)
        hit = jnp.where(slot_row == key_b[g : g + 1] + rank, 1.0, 0.0).astype(BF16)
        bt2[0:width, g * lanes : (g + 1) * lanes] = hit
        bt2[width : 2 * width, g * lanes : (g + 1) * lanes] = hit

    def spread(channels, parts, turned=False):
        for c in range(CHANNELS):
            values = channels[c]
            v8[:, c, :] = values
            v8[:, c + CHANNELS, :] = values
        for g in range(rows):
            mine = owner_row == keys_a[g]
            for p, piece in enumerate(split(v8[g], parts)):
                tall = jnp.concatenate([piece] * (height // 8), axis=0)
                av[p * height : (p + 1) * height, g * lanes : (g + 1) * lanes] = jnp.where(
                    mine, tall, 0.0
                ).astype(BF16)
        if turned:
            wide = matmul(av[0 : parts * height], bt_turned[...])
        else:
            wide = matmul(av[0 : parts * height], bt2[0:width], NT)
        result = wide[0:height]
        for p in range(1, parts):
            result = result + wide[p * height : (p + 1) * height]
        return result

    half = group // 2

    def put_a(target, values):
        for j in range(group):
            target[j] = values[j * CHANNELS : (j + 1) * CHANNELS]

    def get_a(source):
        return jnp.concatenate([source[j] for j in range(group)], axis=0)

    def a_to_b(arrived, target):
        tall = jnp.concatenate(
            [
                arrived[h * half : (h + 1) * half, c, :]
                for h in range(2)
                for c in range(CHANNELS)
            ],
            axis=0,
        )
        target[...] = swap(tall.T.reshape(levels_z, RANKS, height))

    def b_to_a(arrived, target):
        tall = swap(arrived[...]).reshape(width, height).T
        for h in range(2):
            for c in range(CHANNELS):
                at = (h * CHANNELS + c) * half
                target[h * half : (h + 1) * half, c, :] = tall[at : at + half]

    loads[1].wait()
    positions = [pair(positions_ref[k]) for k in range(3)]
    put_a(asend1, spread(positions + [jnp.zeros((rows, lanes), F32)], 3))

    pl.semaphore_wait(barrier, group - 1 + len(near_b))
    for d in (reach, levels_z - reach):
        pl.semaphore_signal(all_in_sem, inc=1, device_id=device_b(on_z[d]), device_id_type=MESH)
    send_a(asend1, arecv1, 0)

    for load in loads[2:]:
        load.wait()
    tall = feat.shape[0]
    b1 = b1_ref[pl.ds(y, 1), :]
    bias_rows = [piece for piece in split(b1, 3)]
    w1_all = jnp.concatenate(
        [w1_own[...].astype(F32)] + bias_rows + [jnp.zeros((tall - enc - 3, hidden), F32)], axis=0
    )
    w1t[...] = (w1_all * 0.5).T.astype(BF16)
    w2t[...] = (w2_own[...].astype(F32) * 0.5).T.astype(BF16)
    w3 = w3_ref[y].astype(F32)
    w3_tall = jnp.concatenate([w3, w3, jnp.zeros((lanes - 2 * CHANNELS, hidden), F32)], axis=0)
    w3t[...] = w3_tall.T[:, 0 : 4 * CHANNELS].astype(BF16)
    w3_rows = jnp.concatenate([w3, jnp.zeros((3 * CHANNELS, hidden), F32)], axis=0).astype(BF16)
    b2_wide[...] = jnp.broadcast_to(b2_ref[pl.ds(y, 1), :] * 0.5, (lanes, hidden)).T
    b3 = column(b3_ref[pl.ds(y, 1), :])
    one_row = lax.broadcasted_iota(jnp.int32, (tall - enc, slots), 0) < 3
    feat[enc:tall, :] = jnp.where(one_row, 1.0, 0.0).astype(BF16)
    act1[hidden:, :] = jnp.ones((act1.shape[0] - hidden, slots), BF16)

    og_sum[...] = jnp.zeros(og_sum.shape, F32)

    for g in range(rows):
        at = slice(g * lanes, (g + 1) * lanes)
        bt_turned[at, :] = bt2[0:width, at].astype(F32).T.astype(BF16)

    wait_a(arecv1, 0)
    a_to_b(arecv1, bsend1)
    pl.semaphore_wait(all_in_sem, 2)
    send_b(bsend1, brecv1, 1, 0)

    lane_tile = height
    level = lax.broadcasted_iota(jnp.int32, (3 * LEVELS, lane_tile), 0) % LEVELS
    half_turns = jnp.left_shift(1, level // 2).astype(F32) * jnp.where(
        level % 2 == 1, 0.5 * math.sqrt(2.0), 0.5
    )
    source_lanes = 2 * lane_tile
    pairs = levels_z // 2 - 1
    own_start, far_start = 2 * pairs * source_lanes, (2 * pairs + 1) * source_lanes
    far = on_z[levels_z // 2]

    def pair_at(d):
        ring = jnp.int32(levels_z)
        return (lax.rem(z + d, ring), lax.rem(z + levels_z - d, ring)), 2 * source_lanes * (d - 1)

    def window(start, count):
        if not isinstance(start, int):
            start = pl.multiple_of(start, source_lanes)
        return pl.ds(start, count * source_lanes)

    def encode(tiles):
        tall_point = jnp.concatenate(
            [
                jnp.concatenate(
                    [
                        jnp.broadcast_to(
                            tile[h * CHANNELS + k : h * CHANNELS + k + 1], (LEVELS, lane_tile)
                        )
                        for k in range(3)
                    ],
                    axis=0,
                )
                for tile in tiles
                for h in range(2)
            ],
            axis=1,
        )
        turns = tall_point * jnp.concatenate([half_turns] * (2 * len(tiles)), axis=1)
        return jnp.concatenate([turns_cosine(turns - 0.25), turns_cosine(turns)], axis=0).astype(
            BF16
        )

    def activate(half, act, slope, at):
        slope[:, at] = half
        active = (half + half * jnp.tanh(half)).astype(BF16)
        act[0:hidden, at] = active
        return active

    def forward(peers, start):
        at = window(start, len(peers))
        feat[0:enc, at] = encode([brecv1[peer] for peer in peers])
        first = activate(matmul(w1t[...], feat[:, at]), act1, slope1, at)
        bias = jnp.concatenate([b2_wide[...]] * (len(peers) * source_lanes // lanes), axis=1)
        second = activate(matmul(w2t[...], first) + bias, act2, slope2, at)
        out = matmul(w3_rows, second)[0:CHANNELS] + b3
        for s, peer in enumerate(peers):
            base = s * source_lanes
            bsend2[peer] = jnp.concatenate(
                [
                    out[:, base : base + lane_tile],
                    out[:, base + lane_tile : base + source_lanes],
                ],
                axis=0,
            )

    def forward_remote(peers, start):
        for peer in peers:
            arrival(brecv1, 0, peer)
        forward(peers, start)
        for peer in peers:
            send(bsend2, brecv2, 2, z, peer, device_b(peer), recv_sem.at[2])

    def forward_pair(d, carry):
        forward_remote(*pair_at(d))
        return carry

    forward([z], own_start)
    lax.fori_loop(1, pairs, forward_pair, 0)
    forward_remote([far], far_start)
    if pairs > 0:
        forward_remote(*pair_at(pairs))

    def slope_step(i, carry):
        at = window(i * source_lanes, 1)
        for slope in (slope1, slope2):
            half = slope[:, at]
            bent = jnp.tanh(half)
            slope[:, at] = ((half + 1.0) - half * bent) * (0.5 * bent + 0.5)
        return carry

    lax.fori_loop(0, levels_z, slope_step, 0)

    lane = lax.broadcasted_iota(jnp.int32, (rows, lanes), 1)
    left = lane < samples

    def per_ray(row):
        tall_row = column(row)
        return jnp.where(left, tall_row[:rows], tall_row[rows:])

    lengths = per_ray(lengths_ref[...].astype(F32))
    tint = [per_ray(color_grad_ref[c : c + 1, :]) for c in range(3)]
    spacing = pair(spacing_ref[...])
    before = lax.broadcasted_iota(jnp.int32, (lanes, lanes), 0)
    after = lax.broadcasted_iota(jnp.int32, (lanes, lanes), 1)
    same_ray = (before // samples) == (after // samples)

    earlier_mask = jnp.where((before < after) & same_ray, 1.0, 0.0).astype(BF16)
    later_mask = jnp.where((before > after) & same_ray, 1.0, 0.0).astype(BF16)

    def scan(values, mask):
        pieces = jnp.concatenate(split(values, 3), axis=0).astype(BF16)
        sums = matmul(pieces, mask)
        return sums[0:rows] + sums[rows : 2 * rows] + sums[2 * rows : 3 * rows]

    live = (lane % samples).astype(F32) < lengths
    brecv2[z] = bsend2[z]
    wait_all(brecv2, levels_z, recv_sem.at[2])
    b_to_a(brecv2, asend2)
    send_a(asend2, arecv2, 3)
    wait_a(arecv2, 3)
    returned = jnp.concatenate(split(get_a(arecv2), 2), axis=1).astype(BF16)
    for g in range(0, rows, 2):
        found = matmul(returned, bt2[:, g * lanes : (g + 2) * lanes])
        for k in range(2):
            kept = jnp.where(
                owner_row == keys_a[g + k], found[:, k * lanes : (k + 1) * lanes], 0.0
            )
            v8[g + k] = jnp.sum(kept.reshape(height // 8, 8, lanes), axis=0)
    field = [v8[:, c, :] + v8[:, c + CHANNELS, :] for c in range(CHANNELS)]

    density = jnp.maximum(field[0], 0.0) + jnp.log1p(jnp.exp(-jnp.abs(field[0])))
    step = jnp.where(live, density * spacing, 0.0)
    left_over = jnp.exp(-step)
    series = step * (
        1.0 - step * (1 / 2) * (1.0 - step * (1 / 3) * (1.0 - step * (1 / 4) * (1.0 - step * (1 / 5))))
    )
    absorbed = jnp.where(step < 0.05, series, 1.0 - left_over)
    trans = jnp.exp(-scan(step, earlier_mask))
    weight = trans * absorbed
    shade = [0.5 + 0.5 * jnp.tanh(0.5 * field[c]) for c in range(1, CHANNELS)]
    seen = tint[0] * shade[0] + tint[1] * shade[1] + tint[2] * shade[2]
    behind = scan(weight * seen, later_mask)
    step_grad = trans * left_over * seen - behind
    density_slope = 0.5 + 0.5 * jnp.tanh(0.5 * field[0])
    out_grad = [jnp.where(live, step_grad * spacing * density_slope, 0.0)]
    for c in range(3):
        out_grad.append(weight * tint[c] * shade[c] * (1.0 - shade[c]))

    put_a(asend3, spread(out_grad, 2, turned=True))
    send_a(asend3, arecv3, 4)
    wait_a(arecv3, 4)
    a_to_b(arecv3, bsend3)
    send_b(bsend3, brecv3, 5, 1)

    def backward_second(peers, start):
        at = window(start, len(peers))
        tiles = [brecv3[peer] for peer in peers]
        for tile in tiles:
            og_sum[...] = og_sum[...] + tile
        grad = jnp.concatenate(
            [tile[h * CHANNELS : (h + 1) * CHANNELS] for tile in tiles for h in range(2)], axis=1
        )
        pieces = jnp.concatenate(
            split(grad, 2) + [jnp.zeros((2 * CHANNELS, grad.shape[1]), F32)], axis=0
        ).astype(BF16)
        og16[:, at] = pieces
        delta = (matmul(w3t[...], pieces) * slope2[:, at]).astype(BF16)
        delta2[:, at] = delta
        return matmul(act1[:, at], delta, NT)

    def backward_pair(d, carry):
        peers, start = pair_at(d)
        for peer in peers:
            arrival(brecv3, 1, peer)
        second_sum[...] = second_sum[...] + backward_second(peers, start)
        return carry

    second_sum[...] = backward_second([z], own_start)
    lax.fori_loop(1, pairs + 1, backward_pair, 0)
    arrival(brecv3, 1, far)
    second = second_sum[...] + backward_second([far], far_start)
    g2_own[...] = second[0:hidden].astype(BF16)

    above, below, across = on_y[1], on_y[copies - 1], on_y[2]

    def at_half(ref, part):
        size = ref.shape[0] // 2
        return ref.at[pl.ds(part * size, size)]

    def move(source, target, index, arrived, peer):
        pltpu.make_async_remote_copy(
            src_ref=source,
            dst_ref=target,
            send_sem=send_sem.at[6 + index],
            recv_sem=arrived,
            device_id={"grp": peer, "cell": cell},
            device_id_type=MESH,
        ).start()

    def share(own, out, index):
        pltpu.make_async_copy(own, out.at[y], own_sem.at[index]).start()
        for up, down in ((0, 1), (1, 0)):
            up_half, down_half = at_half(own, up), at_half(own, down)
            move(up_half, at_half(out.at[y], up), index, ring_sem.at[index, up], above)
            move(down_half, at_half(out.at[y], down), index, ring_sem.at[index, 2 + down], below)

    def landed(out, index, slot, part, block):
        half_ref = at_half(out.at[block], part)
        pltpu.make_async_copy(half_ref, half_ref, ring_sem.at[index, slot]).wait()

    def pass_on(out, index):
        landed(out, index, 0, 0, below)
        half_ref = at_half(out.at[below], 0)
        move(half_ref, half_ref, index, ring_sem.at[index, 4], above)
        landed(out, index, 3, 1, above)
        half_ref = at_half(out.at[above], 1)
        move(half_ref, half_ref, index, ring_sem.at[index, 5], below)

    def gathered(own, out, index):
        pltpu.make_async_copy(own, out.at[y], own_sem.at[index]).wait()
        landed(out, index, 1, 1, below)
        landed(out, index, 2, 0, above)
        landed(out, index, 4, 0, across)
        landed(out, index, 5, 1, across)
        wait_all(out, copies, send_sem.at[6 + index])

    share(g2_own, g2_out, 0)

    step_lanes = 2 * source_lanes

    def backward_first(i, carry):
        at = pl.ds(pl.multiple_of(i * step_lanes, step_lanes), step_lanes)
        delta1[:, at] = (matmul(w2_own[...], delta2[:, at]) * slope1[:, at]).astype(BF16)
        return carry

    lax.fori_loop(0, levels_z // 2, backward_first, 0)
    first = matmul(feat[...], delta1[...], NT)
    g1_own[...] = first[0:enc].astype(BF16)
    share(g1_own, g1_out, 1)
    pass_on(g2_out, 0)
    third = matmul(og16[...], act2[...], NT)
    og_total = jnp.sum(og_sum[...], axis=1, keepdims=True)
    og_total = og_total[0:CHANNELS] + og_total[CHANNELS : 2 * CHANNELS]
    diagonal = lax.broadcasted_iota(jnp.int32, (CHANNELS, hidden), 0) == lax.broadcasted_iota(
        jnp.int32, (CHANNELS, hidden), 1
    )
    third_bias = jnp.sum(
        jnp.where(diagonal, jnp.broadcast_to(og_total, (CHANNELS, hidden)), 0.0),
        axis=0,
        keepdims=True,
    )
    gs_own[...] = jnp.concatenate(
        [
            first[enc : enc + 1],
            second[hidden : hidden + 1],
            third_bias,
            jnp.zeros((1, hidden), F32),
            third[0:CHANNELS] + third[CHANNELS : 2 * CHANNELS],
        ],
        axis=0,
    )
    pltpu.make_async_copy(gs_own, gs_out.at[y], own_sem.at[2]).start()
    for peer in (across, above, below):
        move(gs_own, gs_out.at[y], 2, recv_sem.at[8], peer)
    pass_on(g1_out, 1)

    gathered(g2_own, g2_out, 0)
    gathered(g1_own, g1_out, 1)
    pltpu.make_async_copy(gs_own, gs_out.at[y], own_sem.at[2]).wait()
    wait_all(gs_out, copies, recv_sem.at[8])
    wait_all(gs_out, copies, send_sem.at[8])
    wait_all(asend1, group, send_sem.at[0])
    wait_all(bsend1, levels_z, send_sem.at[1])
    wait_all(bsend2, levels_z, send_sem.at[2])
    wait_all(asend2, group, send_sem.at[3])
    wait_all(asend3, group, send_sem.at[4])
    wait_all(bsend3, levels_z, send_sem.at[5])


def finish(
    g1, g2, gs, g1_out, b1_out, g2_out, b2_out, g3_out, b3_out,
    g1_b, g2_b, gs_b, g1_f, b1_f, g2_f, b2_f, g3_f, b3_f, load_sems, sems
):
    copies = []

    def put(source, target):
        copy = pltpu.make_async_copy(source, target, sems.at[len(copies)])
        copy.start()
        copies.append(copy)

    blocks = g1.shape[0]
    loads = [pltpu.make_async_copy(gs, gs_b, load_sems.at[2 * blocks])]
    for b in range(blocks):
        loads.append(pltpu.make_async_copy(g2.at[b], g2_b.at[b], load_sems.at[2 * b]))
        loads.append(pltpu.make_async_copy(g1.at[b], g1_b.at[b], load_sems.at[2 * b + 1]))
    for load in loads:
        load.start()
    loads[0].wait()
    for b in range(blocks):
        b1_f[b : b + 1, :] = gs_b[b, 0:1, :]
        b2_f[b : b + 1, :] = gs_b[b, 1:2, :]
        g3_f[b] = gs_b[b, 4:8, :]
        b3_f[b : b + 1, :] = gs_b[b, 2:3, 0 : b3_f.shape[1]]
    put(b1_f, b1_out)
    put(b2_f, b2_out)
    put(g3_f, g3_out)
    put(b3_f, b3_out)
    for b in range(blocks):
        loads[1 + 2 * b].wait()
        g2_f[b] = g2_b[b].astype(F32)
        put(g2_f.at[b], g2_out.at[b])
        loads[2 + 2 * b].wait()
        g1_f[b] = g1_b[b].astype(F32)
        put(g1_f.at[b], g1_out.at[b])
    for copy in copies:
        copy.wait()


def local(levels_z, copies, *args):
    (ids, positions, spacing, lengths, color_grad, w1, b1, w2, b2, w3, b3) = args
    rays, samples = spacing.shape
    inner = lax.axis_size("cell") // levels_z
    group = copies * inner
    width = levels_z * RANKS
    height = group * CHANNELS
    slots = group * width
    blocks, enc, hidden = w1.shape
    total = rays * samples
    lanes = 2 * samples
    rows = rays // 2
    tall = enc + 16
    hbm = pl.BlockSpec(memory_space=pltpu.HBM)
    part_a = pltpu.VMEM((group, CHANNELS, width), F32)
    part_b = pltpu.VMEM((levels_z, RANKS, height), F32)
    flops = 2 * slots * (3 * hidden * hidden + 3 * enc * hidden)
    g1, g2, gs = pl.pallas_call(
        functools.partial(kernel, (copies, group, levels_z, rays, samples)),
        out_shape=[
            jax.ShapeDtypeStruct((blocks, enc, hidden), BF16),
            jax.ShapeDtypeStruct((blocks, hidden, hidden), BF16),
            jax.ShapeDtypeStruct((blocks, 8, hidden), F32),
        ],
        in_specs=[hbm] * 11,
        out_specs=[hbm] * 3,
        scratch_shapes=[
            pltpu.VMEM((rays, samples), jnp.int32),
            pltpu.VMEM((3, rays, samples), F32),
            pltpu.VMEM((rays, samples), F32),
            pltpu.VMEM((1, rays), jnp.int32),
            pltpu.VMEM((3, rays), F32),
            pltpu.VMEM(b1.shape, F32),
            pltpu.VMEM(b2.shape, F32),
            pltpu.VMEM(w3.shape, BF16),
            pltpu.VMEM(b3.shape, F32),
            pltpu.VMEM((rows, 8, lanes), F32),
            pltpu.VMEM((3 * height, total), BF16),
            pltpu.VMEM((2 * width, total), BF16),
            pltpu.VMEM((total, width), BF16),
            part_a,
            part_a,
            part_b,
            part_b,
            part_b,
            part_b,
            part_a,
            part_a,
            part_a,
            part_a,
            part_b,
            part_b,
            pltpu.VMEM((tall, slots), BF16),
            pltpu.VMEM((hidden + 16, slots), BF16),
            pltpu.VMEM((hidden, slots), BF16),
            pltpu.VMEM((hidden, slots), F32),
            pltpu.VMEM((hidden, slots), F32),
            pltpu.VMEM((hidden, slots), BF16),
            pltpu.VMEM((hidden, slots), BF16),
            pltpu.VMEM((4 * CHANNELS, slots), BF16),
            pltpu.VMEM((8, height), F32),
            pltpu.VMEM((hidden + 16, hidden), F32),
            pltpu.VMEM((enc, hidden), BF16),
            pltpu.VMEM((hidden, hidden), BF16),
            pltpu.VMEM((hidden, tall), BF16),
            pltpu.VMEM((hidden, hidden), BF16),
            pltpu.VMEM((hidden, 4 * CHANNELS), BF16),
            pltpu.VMEM((hidden, lanes), F32),
            pltpu.VMEM((enc, hidden), BF16),
            pltpu.VMEM((hidden, hidden), BF16),
            pltpu.VMEM((8, hidden), F32),
            pltpu.SemaphoreType.DMA((11,)),
            pltpu.SemaphoreType.DMA((9,)),
            pltpu.SemaphoreType.DMA((9,)),
            pltpu.SemaphoreType.DMA((2, levels_z)),
            pltpu.SemaphoreType.DMA((2, 6)),
            pltpu.SemaphoreType.REGULAR,
            pltpu.SemaphoreType.DMA((3,)),
        ],
        compiler_params=pltpu.CompilerParams(
            collective_id=0, has_side_effects=True, vmem_limit_bytes=VMEM_BYTES
        ),
        cost_estimate=pl.CostEstimate(flops=flops, bytes_accessed=1 << 21, transcendentals=slots * hidden * 2),
    )(
        ids.reshape(rays, samples),
        positions,
        spacing,
        lengths.reshape(1, rays),
        color_grad,
        w1,
        b1,
        w2,
        b2,
        w3,
        b3,
    )
    shapes = [g1.shape, b1.shape, g2.shape, b2.shape, w3.shape, b3.shape]
    return tuple(
        pl.pallas_call(
            finish,
            out_shape=[jax.ShapeDtypeStruct(shape, F32) for shape in shapes],
            in_specs=[hbm] * 3,
            out_specs=[hbm] * 6,
            scratch_shapes=[pltpu.VMEM(piece.shape, piece.dtype) for piece in (g1, g2, gs)]
            + [pltpu.VMEM(shape, F32) for shape in shapes]
            + [
                pltpu.SemaphoreType.DMA((2 * blocks + 1,)),
                pltpu.SemaphoreType.DMA((2 * blocks + 4,)),
            ],
            compiler_params=pltpu.CompilerParams(vmem_limit_bytes=VMEM_BYTES),
        )(g1, g2, gs)
    )


def solution(mesh):
    copies, cells = mesh.shape["grp"], mesh.shape["cell"]
    levels_z = 16 if cells % 16 == 0 and cells >= 128 else 2
    in_specs = (
        P(("grp", "cell"), None, None),
        P(None, ("grp", "cell"), None),
        P(("grp", "cell"), None),
        P(("grp", "cell")),
        P(None, ("grp", "cell")),
        P("cell", None, None),
        P("cell", None),
        P("cell", None, None),
        P("cell", None),
        P("cell", None, None),
        P("cell", None),
    )
    out_specs = (
        P("cell", None, None),
        P("cell", None),
        P("cell", None, None),
        P("cell", None),
        P("cell", None, None),
        P("cell", None),
    )
    return jax.shard_map(
        functools.partial(local, levels_z, copies),
        mesh=mesh,
        in_specs=in_specs,
        out_specs=out_specs,
        check_vma=False,
    )
```

```python
import functools
import math

import jax
import jax.numpy as jnp
from jax import lax
from jax.experimental import pallas as pl
from jax.experimental.pallas import tpu as pltpu
from jax.sharding import PartitionSpec as P

MESH = pl.DeviceIdType.MESH
F32 = jnp.float32
BF16 = jnp.bfloat16

CHANNELS = 4
RANKS = 8
LEVELS = 16
VMEM_BYTES = 64 * 1024 * 1024 - 64 * 1024
SINE = (6.283164044295505, -41.33714237020527, 81.34076885897593, -70.99343300945087)

NN = (((1,), (0,)), ((), ()))
NT = (((1,), (1,)), ((), ()))


def matmul(a, b, dims=NN):
    return lax.dot_general(a, b, dims, preferred_element_type=F32)


def turns_cosine(turns):
    rest = turns - jnp.round(turns)
    w = 0.25 - jnp.abs(rest)
    square = w * w
    poly = SINE[3]
    for coefficient in SINE[2::-1]:
        poly = poly * square + coefficient
    return w * poly


def split(values, parts):
    pieces = []
    for _ in range(parts - 1):
        piece = values.astype(BF16).astype(F32)
        pieces.append(piece)
        values = values - piece
    pieces.append(values)
    return pieces


def column(row):
    n = row.shape[1]
    diagonal = lax.broadcasted_iota(jnp.int32, (n, n), 0) == lax.broadcasted_iota(
        jnp.int32, (n, n), 1
    )
    return jnp.sum(jnp.where(diagonal, jnp.broadcast_to(row, (n, n)), 0.0), axis=1, keepdims=True)


def swap(tiles):
    lanes = tiles.shape[2]
    part = lanes // 8
    sub = lax.broadcasted_iota(jnp.int32, tiles.shape, 1)
    eighth = lax.broadcasted_iota(jnp.int32, tiles.shape, 2) // part
    apart = (eighth - sub) & 7
    result = tiles
    for d in range(1, 8):
        moved = pltpu.roll(pltpu.roll(tiles, 8 - d, 1), d * part, 2)
        result = jnp.where(apart == d, moved, result)
    return result


def kernel(
    sizes,
    ids_hbm,
    positions_hbm,
    spacing_hbm,
    lengths_hbm,
    color_grad_hbm,
    w1_hbm,
    b1_hbm,
    w2_hbm,
    b2_hbm,
    w3_hbm,
    b3_hbm,
    g1_out,
    g2_out,
    gs_out,
    ids_ref,
    positions_ref,
    spacing_ref,
    lengths_ref,
    color_grad_ref,
    b1_ref,
    b2_ref,
    w3_ref,
    b3_ref,
    v8,
    av,
    bt2,
    bt_turned,
    asend1,
    arecv1,
    bsend1,
    brecv1,
    bsend2,
    brecv2,
    asend2,
    arecv2,
    asend3,
    arecv3,
    bsend3,
    brecv3,
    feat,
    act1,
    act2,
    slope1,
    slope2,
    delta1,
    delta2,
    third_sum,
    og_sum,
    second_sum,
    w1_own,
    w2_own,
    w1t,
    w2t,
    w3t,
    b2_wide,
    g1_own,
    g2_own,
    gs_own,
    load_sem,
    send_sem,
    recv_sem,
    near_sem,
    ring_sem,
    all_in_sem,
    own_sem,
):
    copies, group, levels_z, rays, samples = sizes
    inner = group // copies
    lanes = 2 * samples
    rows = rays // 2
    total = rays * samples
    width = levels_z * RANKS
    height = group * CHANNELS
    slots = group * width
    hidden = w2_own.shape[0]
    enc = w1_own.shape[0]

    y = lax.axis_index("grp")
    cell = lax.axis_index("cell")
    z = lax.div(cell, jnp.int32(inner))
    inside = cell - z * inner
    me = y * inner + inside
    cores = 2 if inner % 2 == 0 else 1
    ring_x = inner // cores
    x = lax.div(inside, jnp.int32(cores))
    core = inside - x * cores

    def around(place, count):
        return [place] + [lax.rem(place + d, jnp.int32(count)) for d in range(1, count)]

    def hops(d, count):
        return min(d, count - d)

    on_y, on_x, on_core = around(y, copies), around(x, ring_x), around(core, cores)
    on_z = around(z, levels_z)
    steps_a = sorted(
        ((dy, dx, dc) for dy in range(copies) for dx in range(ring_x) for dc in range(cores)),
        key=lambda d: -hops(d[0], copies) - hops(d[1], ring_x),
    )
    peers_a = [
        (on_y[dy], on_x[dx] * cores + on_core[dc]) for dy, dx, dc in steps_a if dy or dx or dc
    ]
    steps_b = sorted(range(1, levels_z), key=lambda d: -hops(d, levels_z))

    def device_b(peer):
        return {"grp": y, "cell": peer * inner + inside}

    loads = [
        pltpu.make_async_copy(source, target, load_sem.at[i])
        for i, (source, target) in enumerate(
            (
                (ids_hbm, ids_ref),
                (positions_hbm, positions_ref),
                (w2_hbm.at[y], w2_own),
                (w1_hbm.at[y], w1_own),
                (b1_hbm, b1_ref),
                (b2_hbm, b2_ref),
                (w3_hbm, w3_ref),
                (b3_hbm, b3_ref),
                (spacing_hbm, spacing_ref),
                (lengths_hbm, lengths_ref),
                (color_grad_hbm, color_grad_ref),
            )
        )
    ]
    loads[0].start()
    loads[1].start()

    barrier = pltpu.get_barrier_semaphore()
    reach = max(1, levels_z // 4)
    near_b = [d for d in steps_b if hops(d, levels_z) <= reach]
    for d in near_b:
        pl.semaphore_signal(barrier, inc=1, device_id=device_b(on_z[d]), device_id_type=MESH)
    for peer_y, peer_in in peers_a:
        pl.semaphore_signal(
            barrier,
            inc=1,
            device_id={"grp": peer_y, "cell": z * inner + peer_in},
            device_id_type=MESH,
        )
    for load in loads[2:]:
        load.start()
    loads[0].wait()

    def send(source, target, index, own, peer, device, arrived):
        pltpu.make_async_remote_copy(
            src_ref=source.at[peer],
            dst_ref=target.at[own],
            send_sem=send_sem.at[index],
            recv_sem=arrived,
            device_id=device,
            device_id_type=MESH,
        ).start()

    def wait_all(buffer, count, sem):
        others = buffer.at[pl.ds(0, count - 1)]
        pltpu.make_async_copy(others, others, sem).wait()

    def send_a(source, target, index):
        for peer_y, peer_in in peers_a:
            device = {"grp": peer_y, "cell": z * inner + peer_in}
            send(source, target, index, me, peer_y * inner + peer_in, device, recv_sem.at[index])
        target[me] = source[me]

    def wait_a(target, index):
        wait_all(target, group, recv_sem.at[index])

    def send_b(source, target, index, row):
        for d in steps_b:
            send(source, target, index, z, on_z[d], device_b(on_z[d]), near_sem.at[row, z])
        target[z] = source[z]

    def arrival(target, row, peer):
        pltpu.make_async_copy(target.at[peer], target.at[peer], near_sem.at[row, peer]).wait()

    def pair(values):
        return jnp.concatenate([values[:rows], values[rows:]], axis=1)

    ids = pair(ids_ref[...])
    ids_f = ids.astype(F32)
    square = ids_f
    if rows < lanes:
        square = jnp.concatenate([ids_f, jnp.full((lanes - rows, lanes), -1.0, F32)], axis=0)
    columns = square.T
    earlier = lax.broadcasted_iota(jnp.int32, (lanes, lanes), 0) < lax.broadcasted_iota(
        jnp.int32, (lanes, lanes), 1
    )
    id_rows = [ids_f[g : g + 1] for g in range(rows)]
    counts = [jnp.zeros((8, lanes), F32) for _ in range(rows)]
    for first in range(rows):
        wide = jnp.broadcast_to(columns[:, first : first + 1], (lanes, lanes))
        for g in range(first, rows):
            same = wide == id_rows[g]
            if g == first:
                same = same & earlier
            hits = jnp.where(same, 1.0, 0.0)
            counts[g] = counts[g] + jnp.sum(hits.reshape(lanes // 8, 8, lanes), axis=0)
    owner = ids // copies
    key_a = (ids % copies) * inner + owner % inner
    key_b = (owner // inner) * RANKS
    keys_a = [key_a[g : g + 1] for g in range(rows)]
    slot_row = lax.broadcasted_iota(jnp.int32, (width, lanes), 0)
    owner_row = lax.broadcasted_iota(jnp.int32, (height, lanes), 0) // CHANNELS
    for g in range(rows):
        rank = jnp.sum(counts[g], axis=0, keepdims=True).astype(jnp.int32)
        hit = jnp.where(slot_row == key_b[g : g + 1] + rank, 1.0, 0.0).astype(BF16)
        bt2[0:width, g * lanes : (g + 1) * lanes] = hit
        bt2[width : 2 * width, g * lanes : (g + 1) * lanes] = hit

    def spread(channels, parts, turned=False):
        for c in range(CHANNELS):
            values = channels[c]
            v8[:, c, :] = values
            v8[:, c + CHANNELS, :] = values
        for g in range(rows):
            mine = owner_row == keys_a[g]
            for p, piece in enumerate(split(v8[g], parts)):
                tall = jnp.concatenate([piece] * (height // 8), axis=0)
                av[p * height : (p + 1) * height, g * lanes : (g + 1) * lanes] = jnp.where(
                    mine, tall, 0.0
                ).astype(BF16)
        if turned:
            wide = matmul(av[0 : parts * height], bt_turned[...])
        else:
            wide = matmul(av[0 : parts * height], bt2[0:width], NT)
        result = wide[0:height]
        for p in range(1, parts):
            result = result + wide[p * height : (p + 1) * height]
        return result

    half = group // 2

    def put_a(target, values):
        for j in range(group):
            target[j] = values[j * CHANNELS : (j + 1) * CHANNELS]

    def get_a(source):
        return jnp.concatenate([source[j] for j in range(group)], axis=0)

    def a_to_b(arrived, target):
        tall = jnp.concatenate(
            [
                arrived[h * half : (h + 1) * half, c, :]
                for h in range(2)
                for c in range(CHANNELS)
            ],
            axis=0,
        )
        target[...] = swap(tall.T.reshape(levels_z, RANKS, height))

    def b_to_a(arrived, target):
        tall = swap(arrived[...]).reshape(width, height).T
        for h in range(2):
            for c in range(CHANNELS):
                at = (h * CHANNELS + c) * half
                target[h * half : (h + 1) * half, c, :] = tall[at : at + half]

    loads[1].wait()
    positions = [pair(positions_ref[k]) for k in range(3)]
    put_a(asend1, spread(positions + [jnp.zeros((rows, lanes), F32)], 3))

    pl.semaphore_wait(barrier, group - 1 + len(near_b))
    for d in (reach, levels_z - reach):
        pl.semaphore_signal(all_in_sem, inc=1, device_id=device_b(on_z[d]), device_id_type=MESH)
    send_a(asend1, arecv1, 0)

    for load in loads[2:]:
        load.wait()
    tall = feat.shape[0]
    b1 = b1_ref[pl.ds(y, 1), :]
    bias_rows = [piece for piece in split(b1, 3)]
    w1_all = jnp.concatenate(
        [w1_own[...].astype(F32)] + bias_rows + [jnp.zeros((tall - enc - 3, hidden), F32)], axis=0
    )
    w1t[...] = (w1_all * 0.5).T.astype(BF16)
    w2t[...] = (w2_own[...].astype(F32) * 0.5).T.astype(BF16)
    w3 = w3_ref[y].astype(F32)
    w3_tall = jnp.concatenate([w3, w3, jnp.zeros((lanes - 2 * CHANNELS, hidden), F32)], axis=0)
    w3t[...] = w3_tall.T[:, 0 : 4 * CHANNELS].astype(BF16)
    w3_rows = jnp.concatenate([w3, jnp.zeros((3 * CHANNELS, hidden), F32)], axis=0).astype(BF16)
    b2_wide[...] = jnp.broadcast_to(b2_ref[pl.ds(y, 1), :] * 0.5, (lanes, hidden)).T
    b3 = column(b3_ref[pl.ds(y, 1), :])
    one_row = lax.broadcasted_iota(jnp.int32, (tall - enc, slots), 0) < 3
    feat[enc:tall, :] = jnp.where(one_row, 1.0, 0.0).astype(BF16)
    act1[hidden:, :] = jnp.ones((act1.shape[0] - hidden, slots), BF16)

    og_sum[...] = jnp.zeros(og_sum.shape, F32)
    third_sum[...] = jnp.zeros(third_sum.shape, F32)

    for g in range(rows):
        at = slice(g * lanes, (g + 1) * lanes)
        bt_turned[at, :] = bt2[0:width, at].astype(F32).T.astype(BF16)

    wait_a(arecv1, 0)
    a_to_b(arecv1, bsend1)
    pl.semaphore_wait(all_in_sem, 2)
    send_b(bsend1, brecv1, 1, 0)

    lane_tile = height
    level = lax.broadcasted_iota(jnp.int32, (3 * LEVELS, lane_tile), 0) % LEVELS
    half_turns = jnp.left_shift(1, level // 2).astype(F32) * jnp.where(
        level % 2 == 1, 0.5 * math.sqrt(2.0), 0.5
    )
    source_lanes = 2 * lane_tile
    pairs = levels_z // 2 - 1
    own_start, far_start = 2 * pairs * source_lanes, (2 * pairs + 1) * source_lanes
    far = on_z[levels_z // 2]

    def pair_at(d):
        ring = jnp.int32(levels_z)
        return (lax.rem(z + d, ring), lax.rem(z + levels_z - d, ring)), 2 * source_lanes * (d - 1)

    def window(start, count):
        if not isinstance(start, int):
            start = pl.multiple_of(start, source_lanes)
        return pl.ds(start, count * source_lanes)

    def encode(tiles):
        tall_point = jnp.concatenate(
            [
                jnp.concatenate(
                    [
                        jnp.broadcast_to(
                            tile[h * CHANNELS + k : h * CHANNELS + k + 1], (LEVELS, lane_tile)
                        )
                        for k in range(3)
                    ],
                    axis=0,
                )
                for tile in tiles
                for h in range(2)
            ],
            axis=1,
        )
        turns = tall_point * jnp.concatenate([half_turns] * (2 * len(tiles)), axis=1)
        return jnp.concatenate([turns_cosine(turns - 0.25), turns_cosine(turns)], axis=0).astype(
            BF16
        )

    def activate(half, act, slope, at):
        slope[:, at] = half
        active = (half + half * jnp.tanh(half)).astype(BF16)
        act[0:hidden, at] = active
        return active

    def forward(peers, start):
        at = window(start, len(peers))
        feat[0:enc, at] = encode([brecv1[peer] for peer in peers])
        first = activate(matmul(w1t[...], feat[:, at]), act1, slope1, at)
        bias = jnp.concatenate([b2_wide[...]] * (len(peers) * source_lanes // lanes), axis=1)
        second = activate(matmul(w2t[...], first) + bias, act2, slope2, at)
        out = matmul(w3_rows, second)[0:CHANNELS] + b3
        for s, peer in enumerate(peers):
            base = s * source_lanes
            bsend2[peer] = jnp.concatenate(
                [
                    out[:, base : base + lane_tile],
                    out[:, base + lane_tile : base + source_lanes],
                ],
                axis=0,
            )

    def forward_remote(peers, start):
        for peer in peers:
            arrival(brecv1, 0, peer)
        forward(peers, start)
        for peer in peers:
            send(bsend2, brecv2, 2, z, peer, device_b(peer), recv_sem.at[2])

    def forward_pair(d, carry):
        forward_remote(*pair_at(d))
        return carry

    forward([z], own_start)
    lax.fori_loop(1, pairs, forward_pair, 0)
    if pairs > 0:
        forward_remote(*pair_at(pairs))
    forward_remote([far], far_start)

    def slope_step(i, carry):
        at = window(i * source_lanes, 1)
        for slope in (slope1, slope2):
            half = slope[:, at]
            bent = jnp.tanh(half)
            slope[:, at] = ((half + 1.0) - half * bent) * (0.5 * bent + 0.5)
        return carry

    lax.fori_loop(0, levels_z, slope_step, 0)

    lane = lax.broadcasted_iota(jnp.int32, (rows, lanes), 1)
    left = lane < samples

    def per_ray(row):
        tall_row = column(row)
        return jnp.where(left, tall_row[:rows], tall_row[rows:])

    lengths = per_ray(lengths_ref[...].astype(F32))
    tint = [per_ray(color_grad_ref[c : c + 1, :]) for c in range(3)]
    spacing = pair(spacing_ref[...])
    before = lax.broadcasted_iota(jnp.int32, (lanes, lanes), 0)
    after = lax.broadcasted_iota(jnp.int32, (lanes, lanes), 1)
    same_ray = (before // samples) == (after // samples)

    earlier_mask = jnp.where((before < after) & same_ray, 1.0, 0.0).astype(BF16)
    later_mask = jnp.where((before > after) & same_ray, 1.0, 0.0).astype(BF16)

    def scan(values, mask):
        pieces = jnp.concatenate(split(values, 3), axis=0).astype(BF16)
        sums = matmul(pieces, mask)
        return sums[0:rows] + sums[rows : 2 * rows] + sums[2 * rows : 3 * rows]

    live = (lane % samples).astype(F32) < lengths
    brecv2[z] = bsend2[z]
    wait_all(brecv2, levels_z, recv_sem.at[2])
    b_to_a(brecv2, asend2)
    send_a(asend2, arecv2, 3)
    wait_a(arecv2, 3)
    returned = jnp.concatenate(split(get_a(arecv2), 2), axis=1).astype(BF16)
    for g in range(0, rows, 2):
        found = matmul(returned, bt2[:, g * lanes : (g + 2) * lanes])
        for k in range(2):
            kept = jnp.where(
                owner_row == keys_a[g + k], found[:, k * lanes : (k + 1) * lanes], 0.0
            )
            v8[g + k] = jnp.sum(kept.reshape(height // 8, 8, lanes), axis=0)
    field = [v8[:, c, :] + v8[:, c + CHANNELS, :] for c in range(CHANNELS)]

    density = jnp.maximum(field[0], 0.0) + jnp.log1p(jnp.exp(-jnp.abs(field[0])))
    step = jnp.where(live, density * spacing, 0.0)
    left_over = jnp.exp(-step)
    series = step * (
        1.0 - step * (1 / 2) * (1.0 - step * (1 / 3) * (1.0 - step * (1 / 4) * (1.0 - step * (1 / 5))))
    )
    absorbed = jnp.where(step < 0.05, series, 1.0 - left_over)
    trans = jnp.exp(-scan(step, earlier_mask))
    weight = trans * absorbed
    shade = [0.5 + 0.5 * jnp.tanh(0.5 * field[c]) for c in range(1, CHANNELS)]
    seen = tint[0] * shade[0] + tint[1] * shade[1] + tint[2] * shade[2]
    behind = scan(weight * seen, later_mask)
    step_grad = trans * left_over * seen - behind
    density_slope = 0.5 + 0.5 * jnp.tanh(0.5 * field[0])
    out_grad = [jnp.where(live, step_grad * spacing * density_slope, 0.0)]
    for c in range(3):
        out_grad.append(weight * tint[c] * shade[c] * (1.0 - shade[c]))

    put_a(asend3, spread(out_grad, 2, turned=True))
    send_a(asend3, arecv3, 4)
    wait_a(arecv3, 4)
    a_to_b(arecv3, bsend3)
    send_b(bsend3, brecv3, 5, 1)

    def backward_second(peers, start):
        at = window(start, len(peers))
        tiles = [brecv3[peer] for peer in peers]
        for tile in tiles:
            og_sum[...] = og_sum[...] + tile
        grad = jnp.concatenate(
            [tile[h * CHANNELS : (h + 1) * CHANNELS] for tile in tiles for h in range(2)], axis=1
        )
        pieces = jnp.concatenate(
            split(grad, 2) + [jnp.zeros((2 * CHANNELS, grad.shape[1]), F32)], axis=0
        ).astype(BF16)
        delta = (matmul(w3t[...], pieces) * slope2[:, at]).astype(BF16)
        delta2[:, at] = delta
        third_sum[...] = third_sum[...] + matmul(pieces, act2[:, at], NT)
        return matmul(act1[:, at], delta, NT)

    def backward_pair(d, carry):
        peers, start = pair_at(d)
        for peer in peers:
            arrival(brecv3, 1, peer)
        second_sum[...] = second_sum[...] + backward_second(peers, start)
        return carry

    second_sum[...] = backward_second([z], own_start)
    lax.fori_loop(1, pairs + 1, backward_pair, 0)
    arrival(brecv3, 1, far)
    second = second_sum[...] + backward_second([far], far_start)
    g2_own[...] = second[0:hidden].astype(BF16)

    above, below, across = on_y[1], on_y[copies - 1], on_y[2]

    def at_half(ref, part):
        size = ref.shape[0] // 2
        return ref.at[pl.ds(part * size, size)]

    def move(source, target, index, arrived, peer):
        pltpu.make_async_remote_copy(
            src_ref=source,
            dst_ref=target,
            send_sem=send_sem.at[6 + index],
            recv_sem=arrived,
            device_id={"grp": peer, "cell": cell},
            device_id_type=MESH,
        ).start()

    def share(own, out, index):
        pltpu.make_async_copy(own, out.at[y], own_sem.at[index]).start()
        for up, down in ((0, 1), (1, 0)):
            up_half, down_half = at_half(own, up), at_half(own, down)
            move(up_half, at_half(out.at[y], up), index, ring_sem.at[index, up], above)
            move(down_half, at_half(out.at[y], down), index, ring_sem.at[index, 2 + down], below)

    def landed(out, index, slot, part, block):
        half_ref = at_half(out.at[block], part)
        pltpu.make_async_copy(half_ref, half_ref, ring_sem.at[index, slot]).wait()

    def pass_on(out, index):
        landed(out, index, 0, 0, below)
        half_ref = at_half(out.at[below], 0)
        move(half_ref, half_ref, index, ring_sem.at[index, 4], above)
        landed(out, index, 3, 1, above)
        half_ref = at_half(out.at[above], 1)
        move(half_ref, half_ref, index, ring_sem.at[index, 5], below)

    def gathered(own, out, index):
        pltpu.make_async_copy(own, out.at[y], own_sem.at[index]).wait()
        landed(out, index, 1, 1, below)
        landed(out, index, 2, 0, above)
        landed(out, index, 4, 0, across)
        landed(out, index, 5, 1, across)
        wait_all(out, copies, send_sem.at[6 + index])

    share(g2_own, g2_out, 0)

    step_lanes = 2 * source_lanes

    def backward_first(i, carry):
        at = pl.ds(pl.multiple_of(i * step_lanes, step_lanes), step_lanes)
        delta1[:, at] = (matmul(w2_own[...], delta2[:, at]) * slope1[:, at]).astype(BF16)
        return carry

    lax.fori_loop(0, levels_z // 2, backward_first, 0)
    first = matmul(feat[...], delta1[...], NT)
    g1_own[...] = first[0:enc].astype(BF16)
    share(g1_own, g1_out, 1)
    pass_on(g2_out, 0)
    third = third_sum[...]
    og_total = jnp.sum(og_sum[...], axis=1, keepdims=True)
    og_total = og_total[0:CHANNELS] + og_total[CHANNELS : 2 * CHANNELS]
    diagonal = lax.broadcasted_iota(jnp.int32, (CHANNELS, hidden), 0) == lax.broadcasted_iota(
        jnp.int32, (CHANNELS, hidden), 1
    )
    third_bias = jnp.sum(
        jnp.where(diagonal, jnp.broadcast_to(og_total, (CHANNELS, hidden)), 0.0),
        axis=0,
        keepdims=True,
    )
    gs_own[...] = jnp.concatenate(
        [
            first[enc : enc + 1],
            second[hidden : hidden + 1],
            third_bias,
            jnp.zeros((1, hidden), F32),
            third[0:CHANNELS] + third[CHANNELS : 2 * CHANNELS],
        ],
        axis=0,
    )
    pltpu.make_async_copy(gs_own, gs_out.at[y], own_sem.at[2]).start()
    for peer in (across, above, below):
        move(gs_own, gs_out.at[y], 2, recv_sem.at[8], peer)
    pass_on(g1_out, 1)

    gathered(g2_own, g2_out, 0)
    gathered(g1_own, g1_out, 1)
    pltpu.make_async_copy(gs_own, gs_out.at[y], own_sem.at[2]).wait()
    wait_all(gs_out, copies, recv_sem.at[8])
    wait_all(gs_out, copies, send_sem.at[8])
    wait_all(asend1, group, send_sem.at[0])
    wait_all(bsend1, levels_z, send_sem.at[1])
    wait_all(bsend2, levels_z, send_sem.at[2])
    wait_all(asend2, group, send_sem.at[3])
    wait_all(asend3, group, send_sem.at[4])
    wait_all(bsend3, levels_z, send_sem.at[5])


def finish(
    g1, g2, gs, g1_out, b1_out, g2_out, b2_out, g3_out, b3_out,
    g1_b, g2_b, gs_b, g1_f, b1_f, g2_f, b2_f, g3_f, b3_f, load_sems, sems
):
    copies = []

    def put(source, target):
        copy = pltpu.make_async_copy(source, target, sems.at[len(copies)])
        copy.start()
        copies.append(copy)

    blocks = g1.shape[0]
    loads = [pltpu.make_async_copy(gs, gs_b, load_sems.at[2 * blocks])]
    for b in range(blocks):
        loads.append(pltpu.make_async_copy(g2.at[b], g2_b.at[b], load_sems.at[2 * b]))
        loads.append(pltpu.make_async_copy(g1.at[b], g1_b.at[b], load_sems.at[2 * b + 1]))
    for load in loads:
        load.start()
    loads[0].wait()
    for b in range(blocks):
        b1_f[b : b + 1, :] = gs_b[b, 0:1, :]
        b2_f[b : b + 1, :] = gs_b[b, 1:2, :]
        g3_f[b] = gs_b[b, 4:8, :]
        b3_f[b : b + 1, :] = gs_b[b, 2:3, 0 : b3_f.shape[1]]
    put(b1_f, b1_out)
    put(b2_f, b2_out)
    put(g3_f, g3_out)
    put(b3_f, b3_out)
    for b in range(blocks):
        loads[1 + 2 * b].wait()
        g2_f[b] = g2_b[b].astype(F32)
        put(g2_f.at[b], g2_out.at[b])
        loads[2 + 2 * b].wait()
        g1_f[b] = g1_b[b].astype(F32)
        put(g1_f.at[b], g1_out.at[b])
    for copy in copies:
        copy.wait()


def local(levels_z, copies, *args):
    (ids, positions, spacing, lengths, color_grad, w1, b1, w2, b2, w3, b3) = args
    rays, samples = spacing.shape
    inner = lax.axis_size("cell") // levels_z
    group = copies * inner
    width = levels_z * RANKS
    height = group * CHANNELS
    slots = group * width
    blocks, enc, hidden = w1.shape
    total = rays * samples
    lanes = 2 * samples
    rows = rays // 2
    tall = enc + 16
    hbm = pl.BlockSpec(memory_space=pltpu.HBM)
    part_a = pltpu.VMEM((group, CHANNELS, width), F32)
    part_b = pltpu.VMEM((levels_z, RANKS, height), F32)
    flops = 2 * slots * (3 * hidden * hidden + 3 * enc * hidden)
    g1, g2, gs = pl.pallas_call(
        functools.partial(kernel, (copies, group, levels_z, rays, samples)),
        out_shape=[
            jax.ShapeDtypeStruct((blocks, enc, hidden), BF16),
            jax.ShapeDtypeStruct((blocks, hidden, hidden), BF16),
            jax.ShapeDtypeStruct((blocks, 8, hidden), F32),
        ],
        in_specs=[hbm] * 11,
        out_specs=[hbm] * 3,
        scratch_shapes=[
            pltpu.VMEM((rays, samples), jnp.int32),
            pltpu.VMEM((3, rays, samples), F32),
            pltpu.VMEM((rays, samples), F32),
            pltpu.VMEM((1, rays), jnp.int32),
            pltpu.VMEM((3, rays), F32),
            pltpu.VMEM(b1.shape, F32),
            pltpu.VMEM(b2.shape, F32),
            pltpu.VMEM(w3.shape, BF16),
            pltpu.VMEM(b3.shape, F32),
            pltpu.VMEM((rows, 8, lanes), F32),
            pltpu.VMEM((3 * height, total), BF16),
            pltpu.VMEM((2 * width, total), BF16),
            pltpu.VMEM((total, width), BF16),
            part_a,
            part_a,
            part_b,
            part_b,
            part_b,
            part_b,
            part_a,
            part_a,
            part_a,
            part_a,
            part_b,
            part_b,
            pltpu.VMEM((tall, slots), BF16),
            pltpu.VMEM((hidden + 16, slots), BF16),
            pltpu.VMEM((hidden, slots), BF16),
            pltpu.VMEM((hidden, slots), F32),
            pltpu.VMEM((hidden, slots), F32),
            pltpu.VMEM((hidden, slots), BF16),
            pltpu.VMEM((hidden, slots), BF16),
            pltpu.VMEM((4 * CHANNELS, hidden), F32),
            pltpu.VMEM((8, height), F32),
            pltpu.VMEM((hidden + 16, hidden), F32),
            pltpu.VMEM((enc, hidden), BF16),
            pltpu.VMEM((hidden, hidden), BF16),
            pltpu.VMEM((hidden, tall), BF16),
            pltpu.VMEM((hidden, hidden), BF16),
            pltpu.VMEM((hidden, 4 * CHANNELS), BF16),
            pltpu.VMEM((hidden, lanes), F32),
            pltpu.VMEM((enc, hidden), BF16),
            pltpu.VMEM((hidden, hidden), BF16),
            pltpu.VMEM((8, hidden), F32),
            pltpu.SemaphoreType.DMA((11,)),
            pltpu.SemaphoreType.DMA((9,)),
            pltpu.SemaphoreType.DMA((9,)),
            pltpu.SemaphoreType.DMA((2, levels_z)),
            pltpu.SemaphoreType.DMA((2, 6)),
            pltpu.SemaphoreType.REGULAR,
            pltpu.SemaphoreType.DMA((3,)),
        ],
        compiler_params=pltpu.CompilerParams(
            collective_id=0, has_side_effects=True, vmem_limit_bytes=VMEM_BYTES
        ),
        cost_estimate=pl.CostEstimate(flops=flops, bytes_accessed=1 << 21, transcendentals=slots * hidden * 2),
    )(
        ids.reshape(rays, samples),
        positions,
        spacing,
        lengths.reshape(1, rays),
        color_grad,
        w1,
        b1,
        w2,
        b2,
        w3,
        b3,
    )
    shapes = [g1.shape, b1.shape, g2.shape, b2.shape, w3.shape, b3.shape]
    return tuple(
        pl.pallas_call(
            finish,
            out_shape=[jax.ShapeDtypeStruct(shape, F32) for shape in shapes],
            in_specs=[hbm] * 3,
            out_specs=[hbm] * 6,
            scratch_shapes=[pltpu.VMEM(piece.shape, piece.dtype) for piece in (g1, g2, gs)]
            + [pltpu.VMEM(shape, F32) for shape in shapes]
            + [
                pltpu.SemaphoreType.DMA((2 * blocks + 1,)),
                pltpu.SemaphoreType.DMA((2 * blocks + 4,)),
            ],
            compiler_params=pltpu.CompilerParams(vmem_limit_bytes=VMEM_BYTES),
        )(g1, g2, gs)
    )


def solution(mesh):
    copies, cells = mesh.shape["grp"], mesh.shape["cell"]
    levels_z = 16 if cells % 16 == 0 and cells >= 128 else 2
    in_specs = (
        P(("grp", "cell"), None, None),
        P(None, ("grp", "cell"), None),
        P(("grp", "cell"), None),
        P(("grp", "cell")),
        P(None, ("grp", "cell")),
        P("cell", None, None),
        P("cell", None),
        P("cell", None, None),
        P("cell", None),
        P("cell", None, None),
        P("cell", None),
    )
    out_specs = (
        P("cell", None, None),
        P("cell", None),
        P("cell", None, None),
        P("cell", None),
        P("cell", None, None),
        P("cell", None),
    )
    return jax.shard_map(
        functools.partial(local, levels_z, copies),
        mesh=mesh,
        in_specs=in_specs,
        out_specs=out_specs,
        check_vma=False,
    )
```
